32 devices in a mesh: sub: 8 (over z, y), grp: 4 (over x, core).
Axes of the slice: x: 2, y: 2, z: 4, core: 2. Of those that a mesh axis runs over, the one named last changes fastest.
Arguments:
- lam_start: float32 [32768, 128], P(('sub', 'grp')), may hold values from -6 to 6
- loads: float32 [32768, 128], P(('sub', 'grp')), may hold values from -40 to 40
- dual_ops: bfloat16 [32, 1024, 1024], P(('sub', 'grp')), may hold values from -40 to 40, as said below
- modes: float32 [6, 32768], P(None, ('sub', 'grp')), may hold values from -0.6 to 0.6
- coarse_inverse: float32 [192, 192], P('sub', 'grp'), may hold values from -1 to 1, as said below
- face_offset: int32 [8, 4, 8], P(None, 'grp'), may hold values from 0 to 3, as said below
- face_block: int32 [8, 4, 8], P(None, 'grp'), may hold values from 0 to 7
- face_sign: int32 [8, 4, 8], P(None, 'grp'), may hold values from 0 to 1
- contact: int32 [3, 32768], P(None, ('sub', 'grp')), may hold values 0 or 1
Outputs:
- multipliers: float32 [32768, 128], P(('sub', 'grp'))
The draws below stay inside these ranges and needn't reach their ends.
Inputs may be any that keep to these rules, and one draw needn't show every extreme that they name: Each block dual_ops[k] is symmetric positive definite. coarse_inverse is symmetric positive definite. `face_offset`: no face reads from outside the order 0 to 7. For every subdomain no value is taken by more than 4 of its faces, and exactly 4 of its faces share one value.
All inputs are finite; a program needn't handle non-finite values. No bound on the sum of `contact` on one device may be relied on, other than what follows from the above.
Results may differ from the reference program's by a relative error of at most 0.005.
Values may be sent and summed in bfloat16 or wider, within the bound.
No kernel may reach another device: no remote copies, remote signals or barrier semaphores. Data moves between devices by JAX's collectives and lax.ppermute only.
A program may use at most 64 MiB of HBM per device.

```python
import math
import jax
import jax.numpy as jnp
from jax import lax

ORDER = 1024
FACES = 8
FACE_ROWS = 32
CAP = 4
MODES = 6
STEPS = 3
LOADS = 128
SUBS = 32
ROWS = 32768
COARSE_ORDER_SIZE = 192
N_SUB = 8
N_GRP = 4


def draw_dual_ops(key, part):
    keys = jax.random.split(jax.random.fold_in(key, 11), SUBS)

    def one_block(sub_key):
        key_a, key_b = jax.random.split(sub_key, 2)
        base = jax.random.normal(key_a, (ORDER, ORDER), jnp.float32)
        sym = (base + base.T) * (0.7 / math.sqrt(2.0 * ORDER))
        diag = jax.random.uniform(key_b, (ORDER,), jnp.float32, 2.0, 4.0)
        matrix = sym + jnp.diag(diag)
        return matrix.astype(jnp.bfloat16)
    return lax.map(one_block, keys)


def draw_coarse_inverse(key, part):
    key_a, key_b, key_c = jax.random.split(jax.random.fold_in(key, 23), 3)
    half = COARSE_ORDER_SIZE // 2
    base = jax.random.normal(key_a, (COARSE_ORDER_SIZE, COARSE_ORDER_SIZE), jnp.float32)
    sym = (base + base.T) * (0.1 / math.sqrt(2.0 * COARSE_ORDER_SIZE))
    diag = jax.random.uniform(key_b, (COARSE_ORDER_SIZE,), jnp.float32, 0.7, 1.3)
    pair_weight = jax.random.uniform(key_c, (half,), jnp.float32, 0.15, 0.3)
    row_ids = jnp.arange(COARSE_ORDER_SIZE, dtype=jnp.int32)
    pair_row = jnp.concatenate([pair_weight, pair_weight])
    partner = (row_ids + half) % COARSE_ORDER_SIZE
    coupling = jnp.where(partner[:, None] == row_ids[None, :], pair_row[:, None], 0.0)
    return (sym + jnp.diag(diag) + coupling) * (100.0 / ORDER)


def draw_loads(key, part):
    key_a = jax.random.fold_in(jax.random.fold_in(key, 37), 0)
    base = jax.random.normal(key_a, (ROWS, LOADS), jnp.float32)
    sub_pos = (jnp.arange(ROWS) // (ORDER * N_GRP)).astype(jnp.float32)
    rise = jnp.exp(math.log(3.0) * sub_pos / max(N_SUB - 1, 1))
    values = base * rise[:, None]
    return jnp.clip(values, -40.0, 40.0)


def draw_face_offset(key, part):
    key_a, key_b, key_c = jax.random.split(jax.random.fold_in(key, 51), 3)
    steps_tab = jnp.array([-2, -1, 1, 2], jnp.int32)
    sub_pos = jnp.arange(N_SUB, dtype=jnp.int32)[:, None, None]
    target = sub_pos + steps_tab[None, None, :]
    valid = (target >= 0) & (target < N_SUB)
    four = jnp.arange(4, dtype=jnp.int32)
    score = jax.random.randint(key_a, (N_SUB, N_GRP, 4), 0, 1 << 20) * 4 + four
    score = jnp.where(valid, score, -1)
    main = jnp.argmax(score, axis=-1).astype(jnp.int32)
    score_rest = jax.random.randint(key_b, (N_SUB, N_GRP, FACES - CAP, 4), 0, 1 << 20) * 4 + four
    allowed = valid[:, :, None, :] & (four[None, None, None, :] != main[:, :, None, None])
    score_rest = jnp.where(allowed, score_rest, -1)
    rest = jnp.argmax(score_rest, axis=-1).astype(jnp.int32)
    labels = jnp.concatenate([jnp.broadcast_to(main[:, :, None], (N_SUB, N_GRP, CAP)), rest], axis=-1)
    order_key = jax.random.randint(key_c, (N_SUB, N_GRP, FACES), 0, 1 << 20) * FACES + jnp.arange(FACES, dtype=jnp.int32)
    perm = jnp.argsort(order_key, axis=-1)
    return jnp.take_along_axis(labels, perm, axis=-1).astype(jnp.int32)


def place_ends(values, key, least, high):
    longest = values.shape.index(max(values.shape))
    spots = []
    for shift in (0, 1):
        where = [jax.random.randint(jax.random.fold_in(key, axis), (), 0, length) for axis, length in enumerate(values.shape)]
        where[longest] = (where[longest] + shift) % values.shape[longest]
        spots.append(tuple(where))
    return values.at[spots[0]].set(least).at[spots[1]].set(high)


def levels(key, shape, shards, smallest, high):
    def one(position, shards_of):
        heights = jax.random.uniform(jax.random.fold_in(jax.random.fold_in(key, 6), position), (shards_of,), jnp.float32, smallest / len(shards), high / len(shards))
        return jnp.repeat(jnp.exp(heights), shape[position] // shards_of).reshape((-1,) + (1,) * (len(shape) - position - 1))

    loudness = one(*shards[0])
    for cut in shards[1:]:
        loudness = loudness * one(*cut)
    return loudness


def scatter_about(stream_key, dims, spread, bound, shards=(), kind=jnp.bfloat16):
    values = jax.random.normal(stream_key, dims, jnp.float32) * spread
    if len(shards) > 0:
        values = levels(stream_key, dims, shards, -0.22, 0.18) * values
    return jnp.clip(values, min=-bound, max=bound).astype(kind)


def setup_inputs(seed: int = 0) -> dict:
    streams_of = jax.random.split(jax.random.key(seed), 10)
    return {
        "lam_start": scatter_about(streams_of[0], (ROWS, LOADS), 1.0, 6.0, ((0, 32),), jnp.float32),
        "loads": draw_loads(jax.random.fold_in(streams_of[9], 71), 0),
        "dual_ops": draw_dual_ops(jax.random.fold_in(streams_of[9], 71), 0),
        "modes": scatter_about(streams_of[3], (MODES, ROWS), 0.1, 0.6, ((1, 32),), jnp.float32),
        "coarse_inverse": draw_coarse_inverse(jax.random.fold_in(streams_of[9], 71), 0),
        "face_offset": draw_face_offset(jax.random.fold_in(streams_of[9], 71), 0),
        "face_block": place_ends(jax.random.randint(streams_of[6], (N_SUB, N_GRP, FACES), 0, FACES), jax.random.fold_in(streams_of[6], 1), 0, FACES - 1).astype(jnp.int32),
        "face_sign": place_ends(jax.random.randint(streams_of[7], (N_SUB, N_GRP, FACES), 0, 2), jax.random.fold_in(streams_of[7], 1), 0, 1).astype(jnp.int32),
        "contact": place_ends((jax.random.randint(streams_of[8], (STEPS, ROWS), 0, 4) < 1).astype(jnp.int32), jax.random.fold_in(streams_of[8], 1), 0, 1),
    }


def neighbour_maps(face_offset, face_block, face_sign):
    steps_tab = jnp.array([-2, -1, 1, 2], jnp.int32)
    moved = steps_tab[face_offset]
    sub_pos = jnp.arange(N_SUB, dtype=jnp.int32)[:, None, None]
    grp_pos = jnp.arange(N_GRP, dtype=jnp.int32)[None, :, None]
    target = ((sub_pos + moved) * N_GRP + grp_pos).reshape(SUBS, FACES).astype(jnp.int32)
    blocks = face_block.reshape(SUBS, FACES).astype(jnp.int32)
    signs = (2 * face_sign - 1).astype(jnp.float32).reshape(SUBS, FACES)
    return target, blocks, signs


def apply_dual(field, dual_ops, target, blocks, signs):
    normal_loads = field.shape[-1]
    face_total = FACES * FACE_ROWS
    low = field.astype(jnp.bfloat16)
    faces = low[:, :face_total].reshape(SUBS, FACES, FACE_ROWS, normal_loads)
    remote = faces[target, blocks]
    zfaces = (faces.astype(jnp.float32) + signs[:, :, None, None] * remote.astype(jnp.float32)).astype(jnp.bfloat16)
    zfull = jnp.concatenate([zfaces.reshape(SUBS, face_total, normal_loads), low[:, face_total:]], axis=1)

    def one_block(pair):
        return jnp.dot(pair[0].astype(jnp.float32), pair[1].astype(jnp.float32), precision=lax.Precision.HIGHEST)

    image = lax.map(one_block, (dual_ops, zfull)).astype(jnp.bfloat16)
    yfaces = image[:, :face_total].reshape(SUBS, FACES, FACE_ROWS, normal_loads).astype(jnp.float32)
    returned = jnp.zeros((SUBS, FACES, FACE_ROWS, normal_loads), jnp.float32).at[target, blocks].add(signs[:, :, None, None] * yfaces)
    result = image.astype(jnp.float32)
    return result.at[:, :face_total].add(returned.reshape(SUBS, face_total, normal_loads))


def reference(lam_start, loads, dual_ops, modes, coarse_inverse, face_offset, face_block, face_sign, contact):
    target, blocks, signs = neighbour_maps(face_offset, face_block, face_sign)
    normal_loads = lam_start.shape[-1]
    lam = lam_start.reshape(SUBS, ORDER, normal_loads)
    rhs = loads.reshape(SUBS, ORDER, normal_loads)
    coarse_basis_columns = modes.reshape(MODES, SUBS, ORDER)
    for step in range(STEPS):
        dual_gradient = apply_dual(lam, dual_ops, target, blocks, signs) - rhs
        coarse_residual_part = jnp.einsum('vfj,fjy->fvy', coarse_basis_columns, dual_gradient, precision=lax.Precision.HIGHEST).reshape(COARSE_ORDER_SIZE, normal_loads)
        correction_term = jnp.dot(coarse_inverse, coarse_residual_part, precision=lax.Precision.HIGHEST).reshape(SUBS, MODES, normal_loads)
        search_direction = dual_gradient - jnp.einsum('goc,ogh->och', coarse_basis_columns, correction_term, precision=lax.Precision.HIGHEST)
        image = apply_dual(search_direction, dual_ops, target, blocks, signs)
        slope = jnp.sum(dual_gradient * search_direction, axis=(0, 1))
        curv = jnp.sum(search_direction * image, axis=(0, 1))
        alpha = slope / curv
        lam = lam - alpha[None, None, :] * search_direction
        active = contact[step].reshape(SUBS, ORDER)[:, :, None] == 1
        lam = jnp.where(active, jnp.maximum(lam, 0.0), lam)
    return lam.reshape(ROWS, normal_loads)
```

```python
import functools

import jax
import jax.numpy as jnp
from jax import lax
from jax.experimental import pallas as pl
from jax.experimental.pallas import tpu as pltpu
from jax.sharding import PartitionSpec as P

CAP = 4
FACE_ROWS = 32
OFFSETS = (-2, -1, 1, 2)
REACH = ((2, 1), (2, 0), (1, 1), (1, 0))
SWAPS = len(REACH)
DIRECT = (1, 2, 0, 3)
SENDS = ((0, 2), (1, 2), (3,))
PAD = 8
GROUP = 3 * PAD
CONTACT_LANE = GROUP * (1 + len(OFFSETS))
SIDE = 32
FIRST_ROWS = (2 * CAP + 1) * FACE_ROWS
HALF = 64
NEAR = (0, -2, -1, 1, 2)
COARSE = -(-len(NEAR) * PAD // 16) * 16

F32 = jnp.float32
BF16 = jnp.bfloat16


def split(value):
    high = value.astype(BF16)
    return high, (value - high.astype(F32)).astype(BF16)


def partner_of(swap, position, count):
    reach, looks = REACH[swap]
    forward = lax.rem(lax.div(position, reach), 2) == looks
    partner = jnp.where(forward, position + reach, position - reach)
    which = jnp.where(forward, 2 if reach == 1 else 3, 1 if reach == 1 else 0)
    valid = (partner >= 0) & (partner < count)
    return which, jnp.clip(partner, 0, count - 1), valid


def swap_pairs(swap, count):
    reach, looks = REACH[swap]
    pairs = []
    for low in range(count - reach):
        if (low // reach) % 2 == looks:
            pairs += [(low, low + reach), (low + reach, low)]
    return pairs


def swap_direct(sends):
    count = lax.axis_size("sub")
    return [lax.ppermute(send, "sub", swap_pairs(m, count)) for send, m in zip(sends, DIRECT)]


def swap_all(sends):
    count = lax.axis_size("sub")
    here = lax.axis_index("sub")
    even = lax.rem(here + here // 2, 2) == 0
    far, near, beside = [lax.ppermute(send, "sub", swap_pairs(m, count)) for send, m in zip(sends, (0, 1, 3))]
    half = near.shape[0] // 2
    passed = jnp.where(even, near[half:], far[half:])
    return [far, near, lax.ppermute(passed, "sub", swap_pairs(3, count)), beside]


class Table:
    def __init__(self, faces):
        slots = SWAPS * CAP
        self.own_face, self.far_block, self.far_sign = 0, slots, 2 * slots
        self.slot, self.sign, self.offset = 3 * slots, 3 * slots + faces, 3 * slots + 2 * faces
        self.here = 3 * slots + 3 * faces
        self.which = self.here + 2
        self.spare = self.which + SWAPS
        self.size = -(-(self.spare + 1) // 128) * 128


def rows_of(index, rows=FACE_ROWS):
    return pl.ds(pl.multiple_of(index * rows, rows), rows)


def places(sends, span):
    for send, held in zip(sends, SENDS):
        for k, m in enumerate(held):
            yield send, k * span, m


def pack(sends, source, tab, base):
    for send, at, m in places(sends, CAP * FACE_ROWS):
        for j in range(CAP):
            send[at + j * FACE_ROWS:at + (j + 1) * FACE_ROWS, :] = source[rows_of(tab[base + m * CAP + j]), :]


def copies(pairs, sems):
    made = [pltpu.make_async_copy(source, target, sems.at[i]) for i, (source, target) in enumerate(pairs)]
    for copy in made:
        copy.start()
    return made


def build_table(faces, tab, pos, offs, blks, sgns):
    t = Table(faces)
    count = offs.shape[0]
    here = pos[0]
    tab[t.here] = here
    tab[t.here + 1] = pos[1]
    for i in range(3 * SWAPS * CAP):
        tab[i] = 0
    swaps = [partner_of(m, here, count) for m in range(SWAPS)]
    for m, (which, far, valid) in enumerate(swaps):
        tab[t.which + m] = which
        theirs = jnp.int32(0)
        for f in range(faces):
            hit = valid & (offs[far, f] == 3 - which)
            slot = m * CAP + theirs
            tab[jnp.where(hit, t.far_block + slot, t.spare)] = blks[far, f]
            tab[jnp.where(hit, t.far_sign + slot, t.spare)] = 2 * sgns[far, f] - 1
            theirs = theirs + hit.astype(jnp.int32)
    nexts = [jnp.int32(m * CAP) for m in range(SWAPS)]
    for f in range(faces):
        offset = offs[here, f]
        hits = [offset == which for which, _, _ in swaps]
        slot = sum(jnp.where(hit, value, 0) for hit, value in zip(hits, nexts))
        nexts = [value + hit.astype(jnp.int32) for hit, value in zip(hits, nexts)]
        tab[t.own_face + slot] = f
        tab[t.slot + f] = slot
        tab[t.sign + f] = 2 * sgns[here, f] - 1
        tab[t.offset + f] = offset


def widen_slab(slab, groups):
    rows, columns = slab.shape
    modes_n = rows // groups
    blocks = -(-(columns // modes_n * PAD) // HALF)
    source = lax.broadcasted_iota(jnp.int32, (columns, blocks * 128), 0)
    target = lax.broadcasted_iota(jnp.int32, (columns, blocks * 128), 1)
    place = lax.div(source, modes_n) * PAD + lax.rem(source, modes_n)
    place = lax.div(place, HALF) * 128 + lax.rem(place, HALF)
    target_row = lax.broadcasted_iota(jnp.int32, (PAD * groups, rows), 0)
    source_row = lax.broadcasted_iota(jnp.int32, (PAD * groups, rows), 1)
    deepen = (target_row == lax.div(source_row, modes_n) * PAD + lax.rem(source_row, modes_n)).astype(BF16)
    exact = functools.partial(jnp.dot, preferred_element_type=F32)
    high, low = split(slab[...])
    wide = exact(high, (target == place).astype(BF16)) + exact(low, (target == place + HALF).astype(BF16))
    return exact(deepen, wide.astype(BF16)).astype(BF16)


def start_kernel(faces, steps, groups, pos, offs_h, blks_h, sgns_h, lam_h, modes_h, contact_h, slab_h,
                 tab, rows_out, own_t, own_slab, *rest):
    sends, (wide, side, lam, modes, contact, slab, offs, blks, sgns, sems) = rest[:SWAPS], rest[SWAPS:]
    t = Table(faces)
    made = copies(
        ((offs_h, offs), (blks_h, blks), (sgns_h, sgns), (modes_h, modes), (contact_h, contact), (lam_h, lam),
         (slab_h, slab)), sems)
    wide[...] = jnp.zeros_like(wide)
    for copy in made:
        copy.wait()
    build_table(faces, tab, pos, offs, blks, sgns)
    own_slab[...] = widen_slab(slab, groups)

    modes_n = modes.shape[0]
    high, low = split(modes[...])
    high, low = high.astype(F32), low.astype(F32)
    wide[0:modes_n, :] = high
    wide[PAD:PAD + modes_n, :] = low
    rows_out[...] = wide[0:2 * PAD, :].astype(BF16)
    wide[PAD:PAD + modes_n, :] = high
    wide[2 * PAD:2 * PAD + modes_n, :] = low
    wide[CONTACT_LANE:CONTACT_LANE + steps, :] = contact[...].astype(F32)
    own_t[...] = wide[...].T.astype(BF16)

    wide[PAD:3 * PAD, :] = jnp.zeros_like(wide[PAD:3 * PAD, :])
    wide[PAD:PAD + modes_n, :] = low
    wide[2 * PAD:2 * PAD + steps, :] = contact[...].astype(F32)
    wide[CONTACT_LANE:CONTACT_LANE + steps, :] = jnp.zeros_like(contact, F32)
    side[...] = wide[...].T
    block = CAP * FACE_ROWS
    for send, m in zip(sends, DIRECT):
        beside = jnp.zeros((FACE_ROWS, side.shape[1]), F32)
        for j in range(CAP):
            where = rows_of(tab[t.far_block + m * CAP + j])
            lam_high, lam_low = split(lam[where, :])
            here = j * FACE_ROWS
            send[here:here + FACE_ROWS, :] = lam_high
            send[block + here:block + here + FACE_ROWS, :] = lam_low
            beside = beside + (pltpu.roll(side[where, :], SIDE * j, 1) if j else side[where, :])
        send[2 * block:FIRST_ROWS, :] = beside.astype(BF16)
        for k in range(own_slab.shape[1] // 128):
            here = FIRST_ROWS + k * own_slab.shape[0]
            send[here:here + own_slab.shape[0], :] = own_slab[:, k * 128:(k + 1) * 128]


def spread_out(value, out, counts):
    n_sub, n_grp = counts

    def body(i, carry):
        out[pl.ds(i * n_grp, n_grp)] = value
        return carry

    lax.fori_loop(0, n_sub, body, 0, unroll=n_sub <= 8)


def bands(faces, order):
    rows = faces * FACE_ROWS
    return [slice(at, at + rows) for at in range(0, order, rows)]


def fetch(dual_h, inner, sems, faces):
    face_rows = faces * FACE_ROWS
    rest = bands(faces, dual_h.shape[1])[1:]
    return copies([(dual_h.at[0, band], inner.at[band.start - face_rows:band.stop - face_rows]) for band in rest], sems)


def apply(made, dual, inner, zfull, faces):
    field = zfull[...]
    face_rows = faces * FACE_ROWS
    for copy in made:
        copy.wait()
    for band in bands(faces, zfull.shape[0]):
        rows = dual[...] if band.start == 0 else inner[band.start - face_rows:band.stop - face_rows, :]
        yield band, jnp.dot(rows, field, preferred_element_type=F32).astype(BF16)


def gather(field, zfull, tab, faces):
    t = Table(faces)
    order = zfull.shape[0]
    face_rows = faces * FACE_ROWS
    for f in range(faces):
        own = field[f * FACE_ROWS:(f + 1) * FACE_ROWS, :].astype(BF16).astype(F32)
        far = field[order + f * FACE_ROWS:order + (f + 1) * FACE_ROWS, :].astype(BF16).astype(F32)
        zfull[f * FACE_ROWS:(f + 1) * FACE_ROWS, :] = (own + tab[t.sign + f].astype(F32) * far).astype(BF16)
    zfull[face_rows:, :] = field[face_rows:order, :].astype(BF16)


def first_kernel(faces, groups, tab_v, lam_h, own_t, own_slab, dual_h, loads_h, *rest):
    recvs, (lam_all, all_t, zfull, image, dual, loads, choice), rest = rest[:SWAPS], rest[SWAPS:SWAPS + 7], rest[SWAPS + 7:]
    sends, rest = rest[:len(SENDS)], rest[len(SENDS):]
    pieces, (joined, slabs, picked, tab, sems) = rest[:groups], rest[groups:]
    t = Table(faces)
    order, columns = lam_h.shape
    block = CAP * FACE_ROWS
    face_rows = faces * FACE_ROWS
    made = copies(
        ((tab_v, tab), (lam_h, lam_all.at[0:order]), (dual_h.at[0, 0:face_rows], dual), (loads_h.at[0:face_rows], loads)), sems)
    for m, recv in zip(DIRECT, recvs):
        joined[m * FIRST_ROWS:(m + 1) * FIRST_ROWS, :] = recv[0:FIRST_ROWS, :]
    all_t[0:order, :] = own_t[...]
    made[0].wait()
    lanes = all_t.shape[1]
    lane = lax.broadcasted_iota(jnp.int32, (FACE_ROWS, lanes), 1)
    for f in range(faces):
        slot = tab[t.slot + f]
        turn = lax.rem(slot, CAP)
        start = lax.div(slot, CAP) * (2 * CAP + 1)
        high = joined[rows_of(start + turn), :].astype(F32)
        low = joined[rows_of(start + CAP + turn), :].astype(F32)
        at = order + f * FACE_ROWS
        lam_all[at:at + FACE_ROWS, :] = high + low
        side = joined[rows_of(start + 2 * CAP), :].astype(F32)
        mine = side
        for j in range(1, CAP):
            mine = jnp.where(turn == j, pltpu.roll(side, lanes - SIDE * j, 1), mine)
        high = jnp.where(lane < PAD, mine, 0.0)
        low = jnp.where((lane >= PAD) & (lane < 2 * PAD), mine, 0.0)
        flags = jnp.where((lane >= 2 * PAD) & (lane < 3 * PAD), mine, 0.0)
        trio = high + pltpu.roll(high, PAD, 1) + pltpu.roll(low, PAD, 1)
        placed = pltpu.roll(flags, CONTACT_LANE - 2 * PAD, 1)
        for i in range(len(OFFSETS)):
            moved = pltpu.roll(trio, GROUP * (1 + i), 1)
            placed = placed + jnp.where(tab[t.offset + f] == i, moved, 0.0)
        all_t[at:at + FACE_ROWS, :] = placed.astype(BF16)
    height, width = own_slab.shape
    slabs[0] = own_slab[...].astype(F32)
    for m, recv in zip(DIRECT, recvs):
        parts_in = [recv[FIRST_ROWS + k * height:FIRST_ROWS + (k + 1) * height, :] for k in range(width // 128)]
        slabs[1 + tab[t.which + m]] = jnp.concatenate(parts_in, axis=1).astype(F32)
    for i, piece in enumerate(pieces):
        group = lax.rem(tab[t.here + 1] + i, groups)
        picked[...] = jnp.zeros_like(picked)
        for k in range(len(NEAR)):
            picked[k * PAD:(k + 1) * PAD, :] = slabs[k, pl.ds(pl.multiple_of(group * PAD, PAD), PAD), :]
        piece[...] = picked[...].astype(BF16)
    slot = lax.broadcasted_iota(jnp.int32, choice.shape, 1)
    line = lax.broadcasted_iota(jnp.int32, choice.shape, 0)
    inside = lax.rem(slot, FACE_ROWS)
    chosen = jnp.zeros(choice.shape, jnp.int32)
    for q in range(SWAPS * CAP):
        values = jnp.where(line == 0, tab[t.far_block + q] * FACE_ROWS + inside, tab[t.far_sign + q])
        chosen = jnp.where(lax.div(slot, FACE_ROWS) == q, values, chosen)
    choice[...] = chosen.astype(F32)
    made[1].wait()
    gather(lam_all, zfull, tab, faces)
    made[2].wait()
    image[...] = jnp.dot(dual[...], zfull[...], preferred_element_type=F32).astype(BF16)
    pack(sends, image, tab, t.own_face)
    made[3].wait()


def step_length(parts):
    sums = jnp.sum(parts[...], axis=0)
    return sums[0:1, :] / sums[1:2, :]


def stepped(alpha, lam, dirn, all_t, step, rows):
    value = lam[rows, :] - alpha * dirn[rows, :]
    lane = CONTACT_LANE + step
    active = all_t[rows, lane:lane + 1].astype(F32)
    return jnp.where(active > 0.5, jnp.maximum(value, 0.0), value)


def update_kernel(faces, step, tab_v, dual, parts, lam_all, dirn_all, all_t, lam_next, zfull, image, *rest):
    sends, (tab, sems) = rest[:len(SENDS)], rest[len(SENDS):]
    (enter,) = copies(((tab_v, tab),), sems)
    lam_next[...] = stepped(step_length(parts), lam_all, dirn_all, all_t, step, slice(0, lam_all.shape[0]))
    enter.wait()
    gather(lam_next, zfull, tab, faces)
    image[...] = jnp.dot(dual[...], zfull[...], preferred_element_type=F32).astype(BF16)
    pack(sends, image, tab, Table(faces).own_face)


def residual_of(rows, grad):
    high, low = split(grad)
    columns = grad.shape[1]
    prod = jnp.dot(rows, jnp.concatenate([high, low], axis=1), preferred_element_type=F32)
    return prod[0:PAD, 0:columns] + (prod[PAD:2 * PAD, 0:columns] + prod[0:PAD, columns:2 * columns])


def inner_kernel(faces, dual_h, loads_h, zfull, rows, grad, residual, dual, loads, sems):
    order = zfull.shape[0]
    inner = bands(faces, order)[1:]
    face_rows = faces * FACE_ROWS
    made = fetch(dual_h, dual, sems, faces)
    (enter,) = copies(((loads_h.at[face_rows:order], loads),), sems.at[len(made):])
    field = zfull[...]
    enter.wait()
    for copy, band in zip(made, inner):
        copy.wait()
        here = slice(band.start - face_rows, band.stop - face_rows)
        image = jnp.dot(dual[here, :], field, preferred_element_type=F32).astype(BF16)
        grad[here, :] = image.astype(F32) - loads[here, :]
    residual[...] = residual_of(rows[:, face_rows:], grad[...])


def last_kernel(faces, step, parts, lam, dirn, all_t, out_h, out, sems):
    alpha = step_length(parts)
    made = []
    for i, band in enumerate(bands(faces, out.shape[0])):
        out[band, :] = stepped(alpha, lam, dirn, all_t, step, band)
        made += copies([(out.at[band], out_h.at[band])], sems.at[i:])
    for copy in made:
        copy.wait()


def spread_kernel(faces, first, counts, tab_v, choice, image, loads, rows, part, *rest):
    if first:
        pieces, rest = rest[:counts[1]], rest[counts[1]:]
    recvs, (grad, pay_h), rest = rest[:SWAPS], rest[SWAPS:SWAPS + 2], rest[SWAPS + 2:]
    sends, rest = rest[:len(SENDS)], rest[len(SENDS):]
    if first:
        inverse, rest = rest[0], rest[1:]
    if first:
        sorted_, rest = rest[0], rest[1:]
    low_grad, pay, tab, sems = rest
    (enter,) = copies(((tab_v, tab),), sems)
    t = Table(faces)
    n_sub, n_grp = counts
    face_rows = faces * FACE_ROWS
    columns = loads.shape[1]
    line = lax.broadcasted_iota(jnp.int32, (face_rows, choice.shape[1]), 0).astype(F32)
    select = jnp.where(line == choice[0:1, :], choice[1:2, :], 0.0).astype(BF16)
    came = jnp.concatenate([recv[0:CAP * FACE_ROWS, :] for recv in recvs], axis=0)
    returned = jnp.dot(select, came, preferred_element_type=F32)
    grad[...] = image[...].astype(F32) - loads[...] + returned
    low_grad[...] = grad[...].astype(BF16)
    residual = part[...] + residual_of(rows[:, 0:face_rows], grad[...])

    spread_out(jnp.broadcast_to(residual[None], (n_grp,) + residual.shape), pay, counts)
    (leave,) = copies(((pay, pay_h),), sems.at[1:])
    enter.wait()
    pack(sends, low_grad, tab, t.far_block)
    if first:
        inverse[...] = inverse_rows(pieces, tab[t.here + 1], sorted_)
    leave.wait()


def inverse_rows(pieces, group, ordered):
    groups = len(pieces)
    for i, piece in enumerate(pieces):
        ordered[lax.rem(group + groups - i, groups)] = piece[...].astype(F32)
    width = ordered.shape[2]
    blocks = [ordered[g, :, k:k + 128] for g in range(groups) for k in range(0, width, 128)]
    lane = lax.broadcasted_iota(jnp.int32, blocks[0].shape, 1)
    pairs = list(zip(blocks[0::2], blocks[1::2]))
    high = [jnp.where(lane < HALF, one, pltpu.roll(two, HALF, 1)) for one, two in pairs]
    low = [jnp.where(lane < HALF, pltpu.roll(one, HALF, 1), two) for one, two in pairs]
    return jnp.concatenate(high + high + low, axis=1).astype(BF16)


def direction_kernel(faces, tab_v, dual_h, dual, near, grad, grad_in, every, all_t, *rest):
    (far, passed, beside), rest = rest[:SWAPS - 1], rest[SWAPS - 1:]
    recvs = far, near, passed, beside
    (inverse, dirn, parts), rest = rest[:3], rest[3:]
    zfull, joined, grad_all, moved, tab, sems = rest
    (enter,) = copies(((tab_v, tab),), sems)
    made = fetch(dual_h, moved, sems.at[1:], faces)
    t = Table(faces)
    columns = grad.shape[1]
    order = grad.shape[0] + grad_in.shape[0]
    face_rows = faces * FACE_ROWS
    block = CAP * FACE_ROWS
    for m, recv in enumerate(recvs):
        joined[m * block:(m + 1) * block, :] = recv[0:block, :]
    enter.wait()
    for f in range(faces):
        at = f * FACE_ROWS
        grad_all[at:at + FACE_ROWS, :] = joined[rows_of(tab[t.slot + f]), :].astype(F32)
    residual = every[...].reshape(every.shape[0] * PAD, columns)
    high, low = split(residual)
    stacked = jnp.concatenate([high, low, high], axis=0)
    corr = jnp.dot(inverse[...], stacked, preferred_element_type=F32)
    pieces = []
    for k in range(len(NEAR)):
        high, low = split(corr[k * PAD:(k + 1) * PAD, :])
        pieces += [high.astype(F32), low.astype(F32), high.astype(F32)]
    pieces.append(jnp.zeros((all_t.shape[1] - CONTACT_LANE, columns), F32))
    weights = jnp.concatenate(pieces, axis=0).astype(BF16)
    shift = jnp.dot(all_t[...], weights, preferred_element_type=F32)
    dirn[order:, :] = grad_all[...] - shift[order:, :]
    dirn[0:face_rows, :] = grad[...] - shift[0:face_rows, :]
    dirn[face_rows:order, :] = grad_in[...] - shift[face_rows:order, :]
    gather(dirn, zfull, tab, faces)
    curv = jnp.zeros((1, columns), F32)
    for band, product in apply(made, dual, moved, zfull, faces):
        image = product.astype(F32)
        if band.start > 0:
            curv = curv + jnp.sum(dirn[band, :] * image, axis=0, keepdims=True)
            continue
        for f in range(faces):
            at = f * FACE_ROWS
            far = dirn[order + at:order + at + FACE_ROWS, :]
            gathered = dirn[at:at + FACE_ROWS, :] + tab[t.sign + f].astype(F32) * far
            curv = curv + jnp.sum(gathered * image[at:at + FACE_ROWS, :], axis=0, keepdims=True)
    slope = jnp.sum(grad[...] * dirn[0:face_rows, :], axis=0, keepdims=True)
    slope = slope + jnp.sum(grad_in[...] * dirn[face_rows:order, :], axis=0, keepdims=True)
    both = jnp.concatenate([slope, curv], axis=0)
    parts[...] = jnp.broadcast_to(both[None], parts.shape)


SMEM = pltpu.SMEM
VMEM = pltpu.VMEM
HBM = pltpu.HBM


def call(kernel, name, args, outs, scratch=(), scalars=(), copying=0, cost=None):
    size = 0
    held = [(a.shape, a.dtype) for a, space in args if space == VMEM] + [o[:2] for o in outs if o[2] == VMEM]
    for shape, dtype in held + list(scratch):
        shape = (1,) * (2 - len(shape)) + tuple(shape)
        padded = shape[:-2] + (-(-shape[-2] // 16) * 16, -(-shape[-1] // 128) * 128)
        count = jnp.dtype(dtype).itemsize
        for length in padded:
            count *= length
        size += count
    return pl.pallas_call(
        kernel,
        name=name,
        out_shape=[(HBM if space == HBM else jax.ShapeDtypeStruct)(shape, dtype) for shape, dtype, space in outs],
        in_specs=[pl.BlockSpec(memory_space=space) for _, space in args],
        out_specs=[pl.BlockSpec(memory_space=space) for _, _, space in outs],
        scratch_shapes=[pltpu.VMEM(shape, dtype) for shape, dtype in scratch]
        + [pltpu.SMEM(shape, dtype) for shape, dtype in scalars]
        + ([pltpu.SemaphoreType.DMA((copying,))] if copying else []),
        compiler_params=pltpu.CompilerParams(vmem_limit_bytes=size + (6 << 20)),
        cost_estimate=cost,
    )(*[a for a, _ in args])


def vmem(*arrays):
    return [(a, VMEM) for a in arrays]


def hbm(*arrays):
    return [(pltpu.with_memory_space_constraint(a, HBM), HBM) for a in arrays]


def turn(value, ahead):
    count = lax.axis_size("grp")
    return lax.ppermute(value, "grp", [(g, (g + ahead) % count) for g in range(count)])


def exchange(value):
    return lax.all_to_all(value, ("sub", "grp"), 0, 0)


def on_device(
    lam_start, loads, dual_ops, modes, coarse_inverse, face_offset, face_block, face_sign, contact
):
    n_sub, n_grp = lax.axis_size("sub"), lax.axis_size("grp")
    counts = (n_sub, n_grp)
    everyone = n_sub * n_grp
    order, columns = lam_start.shape
    faces = face_offset.shape[-1]
    steps = contact.shape[0]
    halo = faces * FACE_ROWS
    block = CAP * FACE_ROWS
    t = Table(faces)
    modes_n = coarse_inverse.shape[0] // n_grp
    blocks = -(-(coarse_inverse.shape[1] // modes_n * PAD) // HALF)
    slab_shape = (PAD * n_grp, blocks * 128)
    piece = (COARSE, blocks * 128)
    pos = jnp.stack([lax.axis_index("sub"), lax.axis_index("grp")]).astype(jnp.int32)
    flat = hbm(*[a.reshape(n_sub, faces) for a in (face_offset, face_block, face_sign)])
    sent = [((len(held) * block, columns), BF16, VMEM) for held in SENDS]

    tab, rows, own_t, own_slab, *sends = call(
        functools.partial(start_kernel, faces, steps, n_grp), "start",
        [(pos, SMEM)] + flat + hbm(lam_start, modes, contact, coarse_inverse),
        [((t.size,), jnp.int32, SMEM), ((2 * PAD, order), BF16, VMEM), ((order, 128), BF16, VMEM),
         (slab_shape, BF16, VMEM)]
        + [((FIRST_ROWS + slab_shape[0] * slab_shape[1] // 128, columns), BF16, VMEM)] * SWAPS,
        [((128, order), F32), ((order, 128), F32), (lam_start.shape, F32), (modes.shape, F32), (contact.shape, jnp.int32),
         (coarse_inverse.shape, F32)],
        [((n_sub, faces), jnp.int32)] * 3, 7,
    )
    recvs = swap_direct(sends)
    table = [((t.size,), jnp.int32)]
    matrix = ((order - halo, order), BF16)
    parts_n = order // halo
    lam_all, all_t, zfull, image, dual, face_loads, choice, *sends = call(
        functools.partial(first_kernel, faces, n_grp), "first",
        vmem(tab) + hbm(lam_start) + vmem(own_t, own_slab) + hbm(dual_ops, loads) + vmem(*recvs),
        [((order + halo, columns), F32, VMEM), ((order + halo, 128), BF16, VMEM), ((order, columns), BF16, VMEM),
         ((halo, columns), BF16, VMEM), ((halo, order), BF16, VMEM),
         ((halo, columns), F32, VMEM), ((8, SWAPS * block), F32, VMEM)] + sent
        + [(piece, BF16, VMEM)] * n_grp,
        [((SWAPS * FIRST_ROWS, columns), BF16), ((len(NEAR),) + slab_shape, F32), (piece, F32)], table, 4,
    )
    sends, pieces = sends[:len(SENDS)], sends[len(SENDS):]
    for step in range(steps):
        first = step == 0
        returned = swap_all(sends)
        grad_in, part = call(
            functools.partial(inner_kernel, faces), "inner",
            hbm(dual_ops, loads) + vmem(zfull, rows),
            [((order - halo, columns), F32, VMEM), ((PAD, columns), F32, VMEM)],
            [((order - halo, order), BF16), ((order - halo, columns), F32)], (), parts_n,
            pl.CostEstimate(flops=2 * (order - halo) * order * columns, transcendentals=0,
                            bytes_accessed=2 * (order - halo) * order),
        )
        if first:
            pieces = [pieces[0]] + [turn(value, i) for i, value in enumerate(pieces) if i]
        made = [((COARSE, 3 * PAD * everyone), BF16, VMEM)]
        grad, pay, *sends = call(
            functools.partial(spread_kernel, faces, first, counts), "spread",
            vmem(tab, choice, image, face_loads, rows, part, *(pieces if first else []), *returned),
            [((halo, columns), F32, VMEM), ((everyone, PAD, columns), F32, HBM)] + sent + (made if first else []),
            ([((n_grp,) + piece, F32)] if first else []) + [((halo, columns), BF16), ((everyone, PAD, columns), F32)], table, 2,
        )
        if first:
            inverse = sends.pop()
        far, near, passed, beside = swap_all(sends)
        every = exchange(pay)
        dirn, parts = call(
            functools.partial(direction_kernel, faces), "direction",
            vmem(tab) + hbm(dual_ops) + vmem(dual, near, grad, grad_in, every, all_t, far, passed, beside, inverse),
            [((order + halo, columns), F32, VMEM), ((everyone, 2, columns), F32, VMEM)],
            [((order, columns), BF16), ((SWAPS * block, columns), BF16), ((halo, columns), F32), matrix], table, parts_n,
        )
        parts = exchange(parts)
        if step < steps - 1:
            lam_all, zfull, image, *sends = call(
                functools.partial(update_kernel, faces, step), "update",
                vmem(tab, dual, parts, lam_all, dirn, all_t),
                [((order + halo, columns), F32, VMEM), ((order, columns), BF16, VMEM), ((halo, columns), BF16, VMEM)] + sent,
                [], table, 1,
            )
    return call(
        functools.partial(last_kernel, faces, steps - 1), "last",
        vmem(parts, lam_all, dirn, all_t),
        [((order, columns), F32, HBM)], [((order, columns), F32)], (), order // halo,
    )[0]


def solution(mesh):
    return jax.shard_map(
        on_device,
        mesh=mesh,
        in_specs=(
            P(("sub", "grp"), None),
            P(("sub", "grp"), None),
            P(("sub", "grp"), None, None),
            P(None, ("sub", "grp")),
            P("sub", "grp"),
            P(None, "grp", None),
            P(None, "grp", None),
            P(None, "grp", None),
            P(None, ("sub", "grp")),
        ),
        out_specs=P(("sub", "grp"), None),
        check_vma=False,
    )
```

```python
import functools

import jax
import jax.numpy as jnp
from jax import lax
from jax.experimental import pallas as pl
from jax.experimental.pallas import tpu as pltpu
from jax.sharding import PartitionSpec as P

CAP = 4
FACE_ROWS = 32
OFFSETS = (-2, -1, 1, 2)
REACH = ((2, 1), (2, 0), (1, 1), (1, 0))
SWAPS = len(REACH)
DIRECT = (1, 2, 0, 3)
SENDS = ((0, 2), (1, 2), (3,))
PAD = 8
GROUP = 3 * PAD
CONTACT_LANE = GROUP * (1 + len(OFFSETS))
SIDE = 32
FIRST_ROWS = (2 * CAP + 1) * FACE_ROWS
HALF = 64
NEAR = (0, -2, -1, 1, 2)
COARSE = -(-len(NEAR) * PAD // 16) * 16

F32 = jnp.float32
BF16 = jnp.bfloat16


def split(value):
    high = value.astype(BF16)
    return high, (value - high.astype(F32)).astype(BF16)


def partner_of(swap, position, count):
    reach, looks = REACH[swap]
    forward = lax.rem(lax.div(position, reach), 2) == looks
    partner = jnp.where(forward, position + reach, position - reach)
    which = jnp.where(forward, 2 if reach == 1 else 3, 1 if reach == 1 else 0)
    valid = (partner >= 0) & (partner < count)
    return which, jnp.clip(partner, 0, count - 1), valid


def swap_pairs(swap, count):
    reach, looks = REACH[swap]
    pairs = []
    for low in range(count - reach):
        if (low // reach) % 2 == looks:
            pairs += [(low, low + reach), (low + reach, low)]
    return pairs


def swap_direct(sends):
    count = lax.axis_size("sub")
    return [lax.ppermute(send, "sub", swap_pairs(m, count)) for send, m in zip(sends, DIRECT)]


def swap_all(sends):
    count = lax.axis_size("sub")
    here = lax.axis_index("sub")
    even = lax.rem(here + here // 2, 2) == 0
    far, near, beside = [lax.ppermute(send, "sub", swap_pairs(m, count)) for send, m in zip(sends, (0, 1, 3))]
    half = near.shape[0] // 2
    passed = jnp.where(even, near[half:], far[half:])
    return [far, near, lax.ppermute(passed, "sub", swap_pairs(3, count)), beside]


class Table:
    def __init__(self, faces):
        slots = SWAPS * CAP
        self.own_face, self.far_block, self.far_sign = 0, slots, 2 * slots
        self.slot, self.sign, self.offset = 3 * slots, 3 * slots + faces, 3 * slots + 2 * faces
        self.here = 3 * slots + 3 * faces
        self.which = self.here + 2
        self.spare = self.which + SWAPS
        self.size = -(-(self.spare + 1) // 128) * 128


def rows_of(index, rows=FACE_ROWS):
    return pl.ds(pl.multiple_of(index * rows, rows), rows)


def places(sends, span):
    for send, held in zip(sends, SENDS):
        for k, m in enumerate(held):
            yield send, k * span, m


def pack(sends, source, tab, base):
    for send, at, m in places(sends, CAP * FACE_ROWS):
        for j in range(CAP):
            send[at + j * FACE_ROWS:at + (j + 1) * FACE_ROWS, :] = source[rows_of(tab[base + m * CAP + j]), :]


def copies(pairs, sems):
    made = [pltpu.make_async_copy(source, target, sems.at[i]) for i, (source, target) in enumerate(pairs)]
    for copy in made:
        copy.start()
    return made


def build_table(faces, tab, pos, offs, blks, sgns):
    t = Table(faces)
    count = offs.shape[0]
    here = pos[0]
    tab[t.here] = here
    tab[t.here + 1] = pos[1]
    for i in range(3 * SWAPS * CAP):
        tab[i] = 0
    swaps = [partner_of(m, here, count) for m in range(SWAPS)]
    for m, (which, far, valid) in enumerate(swaps):
        tab[t.which + m] = which
        theirs = jnp.int32(0)
        for f in range(faces):
            hit = valid & (offs[far, f] == 3 - which)
            slot = m * CAP + theirs
            tab[jnp.where(hit, t.far_block + slot, t.spare)] = blks[far, f]
            tab[jnp.where(hit, t.far_sign + slot, t.spare)] = 2 * sgns[far, f] - 1
            theirs = theirs + hit.astype(jnp.int32)
    nexts = [jnp.int32(m * CAP) for m in range(SWAPS)]
    for f in range(faces):
        offset = offs[here, f]
        hits = [offset == which for which, _, _ in swaps]
        slot = sum(jnp.where(hit, value, 0) for hit, value in zip(hits, nexts))
        nexts = [value + hit.astype(jnp.int32) for hit, value in zip(hits, nexts)]
        tab[t.own_face + slot] = f
        tab[t.slot + f] = slot
        tab[t.sign + f] = 2 * sgns[here, f] - 1
        tab[t.offset + f] = offset


def widen_slab(slab, groups):
    rows, columns = slab.shape
    modes_n = rows // groups
    blocks = -(-(columns // modes_n * PAD) // HALF)
    source = lax.broadcasted_iota(jnp.int32, (columns, blocks * 128), 0)
    target = lax.broadcasted_iota(jnp.int32, (columns, blocks * 128), 1)
    place = lax.div(source, modes_n) * PAD + lax.rem(source, modes_n)
    place = lax.div(place, HALF) * 128 + lax.rem(place, HALF)
    target_row = lax.broadcasted_iota(jnp.int32, (PAD * groups, rows), 0)
    source_row = lax.broadcasted_iota(jnp.int32, (PAD * groups, rows), 1)
    deepen = (target_row == lax.div(source_row, modes_n) * PAD + lax.rem(source_row, modes_n)).astype(BF16)
    exact = functools.partial(jnp.dot, preferred_element_type=F32)
    high, low = split(slab[...])
    wide = exact(high, (target == place).astype(BF16)) + exact(low, (target == place + HALF).astype(BF16))
    return exact(deepen, wide.astype(BF16)).astype(BF16)


def start_kernel(faces, steps, groups, pos_v, offs_h, blks_h, sgns_h, lam_h, modes_h, contact_h, slab_h,
                 tab_v, rows_out, own_t, own_slab, *rest):
    sends, (wide, side, lam, modes, contact, slab, offs, blks, sgns, pos, tab, sems) = rest[:SWAPS], rest[SWAPS:]
    t = Table(faces)
    made = copies(
        ((offs_h, offs), (blks_h, blks), (sgns_h, sgns), (modes_h, modes), (contact_h, contact), (lam_h, lam),
         (slab_h, slab), (pos_v, pos)), sems)
    wide[...] = jnp.zeros_like(wide)
    for copy in made:
        copy.wait()
    build_table(faces, tab, pos, offs, blks, sgns)
    (leave,) = copies(((tab, tab_v),), sems.at[len(made):])
    own_slab[...] = widen_slab(slab, groups)

    modes_n = modes.shape[0]
    high, low = split(modes[...])
    high, low = high.astype(F32), low.astype(F32)
    wide[0:modes_n, :] = high
    wide[PAD:PAD + modes_n, :] = low
    rows_out[...] = wide[0:2 * PAD, :].astype(BF16)
    wide[PAD:PAD + modes_n, :] = high
    wide[2 * PAD:2 * PAD + modes_n, :] = low
    wide[CONTACT_LANE:CONTACT_LANE + steps, :] = contact[...].astype(F32)
    own_t[...] = wide[...].T.astype(BF16)

    wide[PAD:3 * PAD, :] = jnp.zeros_like(wide[PAD:3 * PAD, :])
    wide[PAD:PAD + modes_n, :] = low
    wide[2 * PAD:2 * PAD + steps, :] = contact[...].astype(F32)
    wide[CONTACT_LANE:CONTACT_LANE + steps, :] = jnp.zeros_like(contact, F32)
    side[...] = wide[...].T
    block = CAP * FACE_ROWS
    for send, m in zip(sends, DIRECT):
        beside = jnp.zeros((FACE_ROWS, side.shape[1]), F32)
        for j in range(CAP):
            where = rows_of(tab[t.far_block + m * CAP + j])
            lam_high, lam_low = split(lam[where, :])
            here = j * FACE_ROWS
            send[here:here + FACE_ROWS, :] = lam_high
            send[block + here:block + here + FACE_ROWS, :] = lam_low
            beside = beside + (pltpu.roll(side[where, :], SIDE * j, 1) if j else side[where, :])
        send[2 * block:FIRST_ROWS, :] = beside.astype(BF16)
        for k in range(own_slab.shape[1] // 128):
            here = FIRST_ROWS + k * own_slab.shape[0]
            send[here:here + own_slab.shape[0], :] = own_slab[:, k * 128:(k + 1) * 128]
    leave.wait()


def spread_out(value, out, counts):
    n_sub, n_grp = counts

    def body(i, carry):
        out[pl.ds(i * n_grp, n_grp)] = value
        return carry

    lax.fori_loop(0, n_sub, body, 0, unroll=n_sub <= 8)


def bands(faces, order):
    rows = faces * FACE_ROWS
    return [slice(at, at + rows) for at in range(0, order, rows)]


def fetch(dual_h, inner, sems, faces):
    face_rows = faces * FACE_ROWS
    rest = bands(faces, dual_h.shape[1])[1:]
    return copies([(dual_h.at[0, band], inner.at[band.start - face_rows:band.stop - face_rows]) for band in rest], sems)


def apply(made, dual, inner, zfull, faces):
    field = zfull[...]
    face_rows = faces * FACE_ROWS
    for copy in made:
        copy.wait()
    for band in bands(faces, zfull.shape[0]):
        rows = dual[...] if band.start == 0 else inner[band.start - face_rows:band.stop - face_rows, :]
        yield band, jnp.dot(rows, field, preferred_element_type=F32).astype(BF16)


def gather(field, zfull, tab, faces):
    t = Table(faces)
    order = zfull.shape[0]
    face_rows = faces * FACE_ROWS
    for f in range(faces):
        own = field[f * FACE_ROWS:(f + 1) * FACE_ROWS, :].astype(BF16).astype(F32)
        far = field[order + f * FACE_ROWS:order + (f + 1) * FACE_ROWS, :].astype(BF16).astype(F32)
        zfull[f * FACE_ROWS:(f + 1) * FACE_ROWS, :] = (own + tab[t.sign + f].astype(F32) * far).astype(BF16)
    zfull[face_rows:, :] = field[face_rows:order, :].astype(BF16)


def first_kernel(faces, groups, tab_v, lam_h, own_t, own_slab, dual_h, loads_h, *rest):
    recvs, (lam_all, all_t, zfull, image, dual, loads, choice), rest = rest[:SWAPS], rest[SWAPS:SWAPS + 7], rest[SWAPS + 7:]
    sends, rest = rest[:len(SENDS)], rest[len(SENDS):]
    pieces, (joined, slabs, picked, tab, sems) = rest[:groups], rest[groups:]
    t = Table(faces)
    order, columns = lam_h.shape
    block = CAP * FACE_ROWS
    face_rows = faces * FACE_ROWS
    made = copies(
        ((tab_v, tab), (lam_h, lam_all.at[0:order]), (dual_h.at[0, 0:face_rows], dual), (loads_h.at[0:face_rows], loads)), sems)
    for m, recv in zip(DIRECT, recvs):
        joined[m * FIRST_ROWS:(m + 1) * FIRST_ROWS, :] = recv[0:FIRST_ROWS, :]
    all_t[0:order, :] = own_t[...]
    made[0].wait()
    lanes = all_t.shape[1]
    lane = lax.broadcasted_iota(jnp.int32, (FACE_ROWS, lanes), 1)
    for f in range(faces):
        slot = tab[t.slot + f]
        turn = lax.rem(slot, CAP)
        start = lax.div(slot, CAP) * (2 * CAP + 1)
        high = joined[rows_of(start + turn), :].astype(F32)
        low = joined[rows_of(start + CAP + turn), :].astype(F32)
        at = order + f * FACE_ROWS
        lam_all[at:at + FACE_ROWS, :] = high + low
        side = joined[rows_of(start + 2 * CAP), :].astype(F32)
        mine = side
        for j in range(1, CAP):
            mine = jnp.where(turn == j, pltpu.roll(side, lanes - SIDE * j, 1), mine)
        high = jnp.where(lane < PAD, mine, 0.0)
        low = jnp.where((lane >= PAD) & (lane < 2 * PAD), mine, 0.0)
        flags = jnp.where((lane >= 2 * PAD) & (lane < 3 * PAD), mine, 0.0)
        trio = high + pltpu.roll(high, PAD, 1) + pltpu.roll(low, PAD, 1)
        placed = pltpu.roll(flags, CONTACT_LANE - 2 * PAD, 1)
        for i in range(len(OFFSETS)):
            moved = pltpu.roll(trio, GROUP * (1 + i), 1)
            placed = placed + jnp.where(tab[t.offset + f] == i, moved, 0.0)
        all_t[at:at + FACE_ROWS, :] = placed.astype(BF16)
    height, width = own_slab.shape
    slabs[0] = own_slab[...].astype(F32)
    for m, recv in zip(DIRECT, recvs):
        parts_in = [recv[FIRST_ROWS + k * height:FIRST_ROWS + (k + 1) * height, :] for k in range(width // 128)]
        slabs[1 + tab[t.which + m]] = jnp.concatenate(parts_in, axis=1).astype(F32)
    for i, piece in enumerate(pieces):
        group = lax.rem(tab[t.here + 1] + i, groups)
        picked[...] = jnp.zeros_like(picked)
        for k in range(len(NEAR)):
            picked[k * PAD:(k + 1) * PAD, :] = slabs[k, pl.ds(pl.multiple_of(group * PAD, PAD), PAD), :]
        piece[...] = picked[...].astype(BF16)
    slot = lax.broadcasted_iota(jnp.int32, choice.shape, 1)
    line = lax.broadcasted_iota(jnp.int32, choice.shape, 0)
    inside = lax.rem(slot, FACE_ROWS)
    chosen = jnp.zeros(choice.shape, jnp.int32)
    for q in range(SWAPS * CAP):
        values = jnp.where(line == 0, tab[t.far_block + q] * FACE_ROWS + inside, tab[t.far_sign + q])
        chosen = jnp.where(lax.div(slot, FACE_ROWS) == q, values, chosen)
    choice[...] = chosen.astype(F32)
    made[1].wait()
    gather(lam_all, zfull, tab, faces)
    made[2].wait()
    image[...] = jnp.dot(dual[...], zfull[...], preferred_element_type=F32).astype(BF16)
    pack(sends, image, tab, t.own_face)
    made[3].wait()


def step_length(parts):
    sums = jnp.sum(parts[...], axis=0)
    return sums[0:1, :] / sums[1:2, :]


def stepped(alpha, lam, dirn, all_t, step, rows):
    value = lam[rows, :] - alpha * dirn[rows, :]
    lane = CONTACT_LANE + step
    active = all_t[rows, lane:lane + 1].astype(F32)
    return jnp.where(active > 0.5, jnp.maximum(value, 0.0), value)


def update_kernel(faces, step, tab_v, dual, parts, lam_all, dirn_all, all_t, lam_next, zfull, image, *rest):
    sends, (tab, sems) = rest[:len(SENDS)], rest[len(SENDS):]
    (enter,) = copies(((tab_v, tab),), sems)
    lam_next[...] = stepped(step_length(parts), lam_all, dirn_all, all_t, step, slice(0, lam_all.shape[0]))
    enter.wait()
    gather(lam_next, zfull, tab, faces)
    image[...] = jnp.dot(dual[...], zfull[...], preferred_element_type=F32).astype(BF16)
    pack(sends, image, tab, Table(faces).own_face)


def residual_of(rows, grad):
    high, low = split(grad)
    columns = grad.shape[1]
    prod = jnp.dot(rows, jnp.concatenate([high, low], axis=1), preferred_element_type=F32)
    return prod[0:PAD, 0:columns] + (prod[PAD:2 * PAD, 0:columns] + prod[0:PAD, columns:2 * columns])


def inner_kernel(faces, dual_h, loads_h, zfull, rows, grad, residual, dual, loads, sems):
    order = zfull.shape[0]
    inner = bands(faces, order)[1:]
    face_rows = faces * FACE_ROWS
    made = fetch(dual_h, dual, sems, faces)
    (enter,) = copies(((loads_h.at[face_rows:order], loads),), sems.at[len(made):])
    field = zfull[...]
    enter.wait()
    for copy, band in zip(made, inner):
        copy.wait()
        here = slice(band.start - face_rows, band.stop - face_rows)
        image = jnp.dot(dual[here, :], field, preferred_element_type=F32).astype(BF16)
        grad[here, :] = image.astype(F32) - loads[here, :]
    residual[...] = residual_of(rows[:, face_rows:], grad[...])


def last_kernel(faces, step, parts, lam, dirn, all_t, out_h, out, sems):
    alpha = step_length(parts)
    made = []
    for i, band in enumerate(bands(faces, out.shape[0])):
        out[band, :] = stepped(alpha, lam, dirn, all_t, step, band)
        made += copies([(out.at[band], out_h.at[band])], sems.at[i:])
    for copy in made:
        copy.wait()


def spread_kernel(faces, first, counts, tab_v, choice, image, loads, rows, part, *rest):
    if first:
        pieces, rest = rest[:counts[1]], rest[counts[1]:]
    recvs, (grad, pay_h), rest = rest[:SWAPS], rest[SWAPS:SWAPS + 2], rest[SWAPS + 2:]
    sends, rest = rest[:len(SENDS)], rest[len(SENDS):]
    if first:
        inverse, rest = rest[0], rest[1:]
    if first:
        sorted_, rest = rest[0], rest[1:]
    low_grad, pay, tab, sems = rest
    (enter,) = copies(((tab_v, tab),), sems)
    t = Table(faces)
    n_sub, n_grp = counts
    face_rows = faces * FACE_ROWS
    columns = loads.shape[1]
    line = lax.broadcasted_iota(jnp.int32, (face_rows, choice.shape[1]), 0).astype(F32)
    select = jnp.where(line == choice[0:1, :], choice[1:2, :], 0.0).astype(BF16)
    came = jnp.concatenate([recv[0:CAP * FACE_ROWS, :] for recv in recvs], axis=0)
    returned = jnp.dot(select, came, preferred_element_type=F32)
    grad[...] = image[...].astype(F32) - loads[...] + returned
    low_grad[...] = grad[...].astype(BF16)
    residual = part[...] + residual_of(rows[:, 0:face_rows], grad[...])

    spread_out(jnp.broadcast_to(residual[None], (n_grp,) + residual.shape), pay, counts)
    (leave,) = copies(((pay, pay_h),), sems.at[1:])
    enter.wait()
    pack(sends, low_grad, tab, t.far_block)
    if first:
        inverse[...] = inverse_rows(pieces, tab[t.here + 1], sorted_)
    leave.wait()


def inverse_rows(pieces, group, ordered):
    groups = len(pieces)
    for i, piece in enumerate(pieces):
        ordered[lax.rem(group + groups - i, groups)] = piece[...].astype(F32)
    width = ordered.shape[2]
    blocks = [ordered[g, :, k:k + 128] for g in range(groups) for k in range(0, width, 128)]
    lane = lax.broadcasted_iota(jnp.int32, blocks[0].shape, 1)
    pairs = list(zip(blocks[0::2], blocks[1::2]))
    high = [jnp.where(lane < HALF, one, pltpu.roll(two, HALF, 1)) for one, two in pairs]
    low = [jnp.where(lane < HALF, pltpu.roll(one, HALF, 1), two) for one, two in pairs]
    return jnp.concatenate(high + high + low, axis=1).astype(BF16)


def direction_kernel(faces, tab_v, dual_h, dual, near, grad, grad_in, every, all_t, *rest):
    (far, passed, beside), rest = rest[:SWAPS - 1], rest[SWAPS - 1:]
    recvs = far, near, passed, beside
    (inverse, dirn, parts), rest = rest[:3], rest[3:]
    zfull, joined, grad_all, moved, tab, sems = rest
    (enter,) = copies(((tab_v, tab),), sems)
    made = fetch(dual_h, moved, sems.at[1:], faces)
    t = Table(faces)
    columns = grad.shape[1]
    order = grad.shape[0] + grad_in.shape[0]
    face_rows = faces * FACE_ROWS
    block = CAP * FACE_ROWS
    for m, recv in enumerate(recvs):
        joined[m * block:(m + 1) * block, :] = recv[0:block, :]
    enter.wait()
    for f in range(faces):
        at = f * FACE_ROWS
        grad_all[at:at + FACE_ROWS, :] = joined[rows_of(tab[t.slot + f]), :].astype(F32)
    residual = every[...].reshape(every.shape[0] * PAD, columns)
    high, low = split(residual)
    stacked = jnp.concatenate([high, low, high], axis=0)
    corr = jnp.dot(inverse[...], stacked, preferred_element_type=F32)
    pieces = []
    for k in range(len(NEAR)):
        high, low = split(corr[k * PAD:(k + 1) * PAD, :])
        pieces += [high.astype(F32), low.astype(F32), high.astype(F32)]
    pieces.append(jnp.zeros((all_t.shape[1] - CONTACT_LANE, columns), F32))
    weights = jnp.concatenate(pieces, axis=0).astype(BF16)
    shift = jnp.dot(all_t[...], weights, preferred_element_type=F32)
    dirn[order:, :] = grad_all[...] - shift[order:, :]
    dirn[0:face_rows, :] = grad[...] - shift[0:face_rows, :]
    dirn[face_rows:order, :] = grad_in[...] - shift[face_rows:order, :]
    gather(dirn, zfull, tab, faces)
    curv = jnp.zeros((1, columns), F32)
    for band, product in apply(made, dual, moved, zfull, faces):
        image = product.astype(F32)
        if band.start > 0:
            curv = curv + jnp.sum(dirn[band, :] * image, axis=0, keepdims=True)
            continue
        for f in range(faces):
            at = f * FACE_ROWS
            far = dirn[order + at:order + at + FACE_ROWS, :]
            gathered = dirn[at:at + FACE_ROWS, :] + tab[t.sign + f].astype(F32) * far
            curv = curv + jnp.sum(gathered * image[at:at + FACE_ROWS, :], axis=0, keepdims=True)
    slope = jnp.sum(grad[...] * dirn[0:face_rows, :], axis=0, keepdims=True)
    slope = slope + jnp.sum(grad_in[...] * dirn[face_rows:order, :], axis=0, keepdims=True)
    both = jnp.concatenate([slope, curv], axis=0)
    parts[...] = jnp.broadcast_to(both[None], parts.shape)


SMEM = pltpu.SMEM
VMEM = pltpu.VMEM
HBM = pltpu.HBM


def call(kernel, name, args, outs, scratch=(), scalars=(), copying=0, cost=None):
    size = 0
    held = [(a.shape, a.dtype) for a, space in args if space == VMEM] + [o[:2] for o in outs if o[2] == VMEM]
    for shape, dtype in held + list(scratch):
        shape = (1,) * (2 - len(shape)) + tuple(shape)
        padded = shape[:-2] + (-(-shape[-2] // 16) * 16, -(-shape[-1] // 128) * 128)
        count = jnp.dtype(dtype).itemsize
        for length in padded:
            count *= length
        size += count
    return pl.pallas_call(
        kernel,
        name=name,
        out_shape=[(HBM if space == HBM else jax.ShapeDtypeStruct)(shape, dtype) for shape, dtype, space in outs],
        in_specs=[pl.BlockSpec(memory_space=space) for _, space in args],
        out_specs=[pl.BlockSpec(memory_space=space) for _, _, space in outs],
        scratch_shapes=[pltpu.VMEM(shape, dtype) for shape, dtype in scratch]
        + [pltpu.SMEM(shape, dtype) for shape, dtype in scalars]
        + ([pltpu.SemaphoreType.DMA((copying,))] if copying else []),
        compiler_params=pltpu.CompilerParams(vmem_limit_bytes=size + (6 << 20)),
        cost_estimate=cost,
    )(*[a for a, _ in args])


def vmem(*arrays):
    return [(a, VMEM) for a in arrays]


def hbm(*arrays):
    return [(pltpu.with_memory_space_constraint(a, HBM), HBM) for a in arrays]


def turn(value, ahead):
    count = lax.axis_size("grp")
    return lax.ppermute(value, "grp", [(g, (g + ahead) % count) for g in range(count)])


def exchange(value):
    return lax.all_to_all(value, ("sub", "grp"), 0, 0)


def on_device(
    lam_start, loads, dual_ops, modes, coarse_inverse, face_offset, face_block, face_sign, contact
):
    n_sub, n_grp = lax.axis_size("sub"), lax.axis_size("grp")
    counts = (n_sub, n_grp)
    everyone = n_sub * n_grp
    order, columns = lam_start.shape
    faces = face_offset.shape[-1]
    steps = contact.shape[0]
    halo = faces * FACE_ROWS
    block = CAP * FACE_ROWS
    t = Table(faces)
    modes_n = coarse_inverse.shape[0] // n_grp
    blocks = -(-(coarse_inverse.shape[1] // modes_n * PAD) // HALF)
    slab_shape = (PAD * n_grp, blocks * 128)
    piece = (COARSE, blocks * 128)
    lane = jnp.arange(128, dtype=jnp.int32)
    pos = jnp.where(lane == 0, lax.axis_index("sub"), jnp.where(lane == 1, lax.axis_index("grp"), 0)).astype(jnp.int32)
    flat = hbm(*[a.reshape(n_sub, faces) for a in (face_offset, face_block, face_sign)])
    sent = [((len(held) * block, columns), BF16, VMEM) for held in SENDS]

    tab, rows, own_t, own_slab, *sends = call(
        functools.partial(start_kernel, faces, steps, n_grp), "start",
        vmem(pos) + flat + hbm(lam_start, modes, contact, coarse_inverse),
        [((t.size,), jnp.int32, VMEM), ((2 * PAD, order), BF16, VMEM), ((order, 128), BF16, VMEM),
         (slab_shape, BF16, VMEM)]
        + [((FIRST_ROWS + slab_shape[0] * slab_shape[1] // 128, columns), BF16, VMEM)] * SWAPS,
        [((128, order), F32), ((order, 128), F32), (lam_start.shape, F32), (modes.shape, F32), (contact.shape, jnp.int32),
         (coarse_inverse.shape, F32)],
        [((n_sub, faces), jnp.int32)] * 3 + [((128,), jnp.int32), ((t.size,), jnp.int32)], 9,
    )
    recvs = swap_direct(sends)
    table = [((t.size,), jnp.int32)]
    matrix = ((order - halo, order), BF16)
    parts_n = order // halo
    lam_all, all_t, zfull, image, dual, face_loads, choice, *sends = call(
        functools.partial(first_kernel, faces, n_grp), "first",
        vmem(tab) + hbm(lam_start) + vmem(own_t, own_slab) + hbm(dual_ops, loads) + vmem(*recvs),
        [((order + halo, columns), F32, VMEM), ((order + halo, 128), BF16, VMEM), ((order, columns), BF16, VMEM),
         ((halo, columns), BF16, VMEM), ((halo, order), BF16, VMEM),
         ((halo, columns), F32, VMEM), ((8, SWAPS * block), F32, VMEM)] + sent
        + [(piece, BF16, VMEM)] * n_grp,
        [((SWAPS * FIRST_ROWS, columns), BF16), ((len(NEAR),) + slab_shape, F32), (piece, F32)], table, 4,
    )
    sends, pieces = sends[:len(SENDS)], sends[len(SENDS):]
    for step in range(steps):
        first = step == 0
        returned = swap_all(sends)
        grad_in, part = call(
            functools.partial(inner_kernel, faces), "inner",
            hbm(dual_ops, loads) + vmem(zfull, rows),
            [((order - halo, columns), F32, VMEM), ((PAD, columns), F32, VMEM)],
            [((order - halo, order), BF16), ((order - halo, columns), F32)], (), parts_n,
            pl.CostEstimate(flops=2 * (order - halo) * order * columns, transcendentals=0,
                            bytes_accessed=2 * (order - halo) * order),
        )
        if first:
            pieces = [pieces[0]] + [turn(value, i) for i, value in enumerate(pieces) if i]
        made = [((COARSE, 3 * PAD * everyone), BF16, VMEM)]
        grad, pay, *sends = call(
            functools.partial(spread_kernel, faces, first, counts), "spread",
            vmem(tab, choice, image, face_loads, rows, part, *(pieces if first else []), *returned),
            [((halo, columns), F32, VMEM), ((everyone, PAD, columns), F32, HBM)] + sent + (made if first else []),
            ([((n_grp,) + piece, F32)] if first else []) + [((halo, columns), BF16), ((everyone, PAD, columns), F32)], table, 2,
        )
        if first:
            inverse = sends.pop()
        far, near, passed, beside = swap_all(sends)
        every = exchange(pay)
        dirn, parts = call(
            functools.partial(direction_kernel, faces), "direction",
            vmem(tab) + hbm(dual_ops) + vmem(dual, near, grad, grad_in, every, all_t, far, passed, beside, inverse),
            [((order + halo, columns), F32, VMEM), ((everyone, 2, columns), F32, VMEM)],
            [((order, columns), BF16), ((SWAPS * block, columns), BF16), ((halo, columns), F32), matrix], table, parts_n,
        )
        parts = exchange(parts)
        if step < steps - 1:
            lam_all, zfull, image, *sends = call(
                functools.partial(update_kernel, faces, step), "update",
                vmem(tab, dual, parts, lam_all, dirn, all_t),
                [((order + halo, columns), F32, VMEM), ((order, columns), BF16, VMEM), ((halo, columns), BF16, VMEM)] + sent,
                [], table, 1,
            )
    return call(
        functools.partial(last_kernel, faces, steps - 1), "last",
        vmem(parts, lam_all, dirn, all_t),
        [((order, columns), F32, HBM)], [((order, columns), F32)], (), order // halo,
    )[0]


def solution(mesh):
    return jax.shard_map(
        on_device,
        mesh=mesh,
        in_specs=(
            P(("sub", "grp"), None),
            P(("sub", "grp"), None),
            P(("sub", "grp"), None, None),
            P(None, ("sub", "grp")),
            P("sub", "grp"),
            P(None, "grp", None),
            P(None, "grp", None),
            P(None, "grp", None),
            P(None, ("sub", "grp")),
        ),
        out_specs=P(("sub", "grp"), None),
        check_vma=False,
    )
```

```python
import functools

import jax
import jax.numpy as jnp
from jax import lax
from jax.experimental import pallas as pl
from jax.experimental.pallas import tpu as pltpu
from jax.sharding import PartitionSpec as P

CAP = 4
FACE_ROWS = 32
OFFSETS = (-2, -1, 1, 2)
REACH = ((2, 1), (2, 0), (1, 1), (1, 0))
SWAPS = len(REACH)
DIRECT = (1, 2, 0, 3)
SENDS = ((0, 2), (1, 2), (3,))
PAD = 8
GROUP = 3 * PAD
CONTACT_LANE = GROUP * (1 + len(OFFSETS))
SIDE = 32
FIRST_ROWS = (2 * CAP + 1) * FACE_ROWS
HALF = 64
NEAR = (0, -2, -1, 1, 2)
COARSE = -(-len(NEAR) * PAD // 16) * 16

F32 = jnp.float32
BF16 = jnp.bfloat16


def split(value):
    high = value.astype(BF16)
    return high, (value - high.astype(F32)).astype(BF16)


def partner_of(swap, position, count):
    reach, looks = REACH[swap]
    forward = lax.rem(lax.div(position, reach), 2) == looks
    partner = jnp.where(forward, position + reach, position - reach)
    which = jnp.where(forward, 2 if reach == 1 else 3, 1 if reach == 1 else 0)
    valid = (partner >= 0) & (partner < count)
    return which, jnp.clip(partner, 0, count - 1), valid


def swap_pairs(swap, count):
    reach, looks = REACH[swap]
    pairs = []
    for low in range(count - reach):
        if (low // reach) % 2 == looks:
            pairs += [(low, low + reach), (low + reach, low)]
    return pairs


def swap_direct(sends):
    count = lax.axis_size("sub")
    return [lax.ppermute(send, "sub", swap_pairs(m, count)) for send, m in zip(sends, DIRECT)]


def swap_all(sends):
    count = lax.axis_size("sub")
    here = lax.axis_index("sub")
    even = lax.rem(here + here // 2, 2) == 0
    far, near, beside = [lax.ppermute(send, "sub", swap_pairs(m, count)) for send, m in zip(sends, (0, 1, 3))]
    half = near.shape[0] // 2
    passed = jnp.where(even, near[half:], far[half:])
    return [far, near, lax.ppermute(passed, "sub", swap_pairs(3, count)), beside]


class Table:
    def __init__(self, faces):
        slots = SWAPS * CAP
        self.own_face, self.far_block, self.far_sign = 0, slots, 2 * slots
        self.slot, self.sign, self.offset = 3 * slots, 3 * slots + faces, 3 * slots + 2 * faces
        self.here = 3 * slots + 3 * faces
        self.which = self.here + 2
        self.spare = self.which + SWAPS
        self.size = -(-(self.spare + 1) // 128) * 128


def rows_of(index, rows=FACE_ROWS):
    return pl.ds(pl.multiple_of(index * rows, rows), rows)


def places(sends, span):
    for send, held in zip(sends, SENDS):
        for k, m in enumerate(held):
            yield send, k * span, m


def pack(sends, source, tab, base):
    for send, at, m in places(sends, CAP * FACE_ROWS):
        for j in range(CAP):
            send[at + j * FACE_ROWS:at + (j + 1) * FACE_ROWS, :] = source[rows_of(tab[base + m * CAP + j]), :]


def copies(pairs, sems):
    made = [pltpu.make_async_copy(source, target, sems.at[i]) for i, (source, target) in enumerate(pairs)]
    for copy in made:
        copy.start()
    return made


def build_table(faces, tab, pos, offs, blks, sgns):
    t = Table(faces)
    count = offs.shape[0]
    here = pos[0]
    tab[t.here] = here
    tab[t.here + 1] = pos[1]
    for i in range(3 * SWAPS * CAP):
        tab[i] = 0
    swaps = [partner_of(m, here, count) for m in range(SWAPS)]
    for m, (which, far, valid) in enumerate(swaps):
        tab[t.which + m] = which
        theirs = jnp.int32(0)
        for f in range(faces):
            hit = valid & (offs[far, f] == 3 - which)
            slot = m * CAP + theirs
            tab[jnp.where(hit, t.far_block + slot, t.spare)] = blks[far, f]
            tab[jnp.where(hit, t.far_sign + slot, t.spare)] = 2 * sgns[far, f] - 1
            theirs = theirs + hit.astype(jnp.int32)
    nexts = [jnp.int32(m * CAP) for m in range(SWAPS)]
    for f in range(faces):
        offset = offs[here, f]
        hits = [offset == which for which, _, _ in swaps]
        slot = sum(jnp.where(hit, value, 0) for hit, value in zip(hits, nexts))
        nexts = [value + hit.astype(jnp.int32) for hit, value in zip(hits, nexts)]
        tab[t.own_face + slot] = f
        tab[t.slot + f] = slot
        tab[t.sign + f] = 2 * sgns[here, f] - 1
        tab[t.offset + f] = offset


def widen_slab(slab, groups):
    rows, columns = slab.shape
    modes_n = rows // groups
    blocks = -(-(columns // modes_n * PAD) // HALF)
    source = lax.broadcasted_iota(jnp.int32, (columns, blocks * 128), 0)
    target = lax.broadcasted_iota(jnp.int32, (columns, blocks * 128), 1)
    place = lax.div(source, modes_n) * PAD + lax.rem(source, modes_n)
    place = lax.div(place, HALF) * 128 + lax.rem(place, HALF)
    target_row = lax.broadcasted_iota(jnp.int32, (PAD * groups, rows), 0)
    source_row = lax.broadcasted_iota(jnp.int32, (PAD * groups, rows), 1)
    deepen = (target_row == lax.div(source_row, modes_n) * PAD + lax.rem(source_row, modes_n)).astype(BF16)
    exact = functools.partial(jnp.dot, preferred_element_type=F32)
    high, low = split(slab[...])
    wide = exact(high, (target == place).astype(BF16)) + exact(low, (target == place + HALF).astype(BF16))
    return exact(deepen, wide.astype(BF16)).astype(BF16)


def start_kernel(faces, steps, groups, pos_v, offs_h, blks_h, sgns_h, lam_h, modes_h, contact_h, slab_h,
                 tab_v, rows_out, own_t, own_slab, *rest):
    sends, (wide, side, lam, modes, contact, slab, offs, blks, sgns, pos, tab, sems) = rest[:SWAPS], rest[SWAPS:]
    t = Table(faces)
    made = copies(
        ((offs_h, offs), (blks_h, blks), (sgns_h, sgns), (modes_h, modes), (contact_h, contact), (lam_h, lam),
         (slab_h, slab), (pos_v, pos)), sems)
    wide[...] = jnp.zeros_like(wide)
    for copy in made:
        copy.wait()
    build_table(faces, tab, pos, offs, blks, sgns)
    (leave,) = copies(((tab, tab_v),), sems.at[len(made):])
    own_slab[...] = widen_slab(slab, groups)

    modes_n = modes.shape[0]
    high, low = split(modes[...])
    high, low = high.astype(F32), low.astype(F32)
    wide[0:modes_n, :] = high
    wide[PAD:PAD + modes_n, :] = low
    rows_out[...] = wide[0:2 * PAD, :].astype(BF16)
    wide[PAD:PAD + modes_n, :] = high
    wide[2 * PAD:2 * PAD + modes_n, :] = low
    wide[CONTACT_LANE:CONTACT_LANE + steps, :] = contact[...].astype(F32)
    own_t[...] = wide[...].T.astype(BF16)

    wide[PAD:3 * PAD, :] = jnp.zeros_like(wide[PAD:3 * PAD, :])
    wide[PAD:PAD + modes_n, :] = low
    wide[2 * PAD:2 * PAD + steps, :] = contact[...].astype(F32)
    wide[CONTACT_LANE:CONTACT_LANE + steps, :] = jnp.zeros_like(contact, F32)
    side[...] = wide[...].T
    block = CAP * FACE_ROWS
    for send, m in zip(sends, DIRECT):
        beside = jnp.zeros((FACE_ROWS, side.shape[1]), F32)
        for j in range(CAP):
            where = rows_of(tab[t.far_block + m * CAP + j])
            lam_high, lam_low = split(lam[where, :])
            here = j * FACE_ROWS
            send[here:here + FACE_ROWS, :] = lam_high
            send[block + here:block + here + FACE_ROWS, :] = lam_low
            beside = beside + (pltpu.roll(side[where, :], SIDE * j, 1) if j else side[where, :])
        send[2 * block:FIRST_ROWS, :] = beside.astype(BF16)
        for k in range(own_slab.shape[1] // 128):
            here = FIRST_ROWS + k * own_slab.shape[0]
            send[here:here + own_slab.shape[0], :] = own_slab[:, k * 128:(k + 1) * 128]
    leave.wait()


def spread_out(value, out, counts):
    n_sub, n_grp = counts

    def body(i, carry):
        out[pl.ds(i * n_grp, n_grp)] = value
        return carry

    lax.fori_loop(0, n_sub, body, 0, unroll=n_sub <= 8)


def bands(faces, order):
    rows = faces * FACE_ROWS
    return [slice(at, at + rows) for at in range(0, order, rows)]


def fetch(dual_h, inner, sems, faces):
    face_rows = faces * FACE_ROWS
    rest = bands(faces, dual_h.shape[1])[1:]
    return copies([(dual_h.at[0, band], inner.at[band.start - face_rows:band.stop - face_rows]) for band in rest], sems)


def apply(made, dual, inner, zfull, faces):
    field = zfull[...]
    face_rows = faces * FACE_ROWS
    for copy in made:
        copy.wait()
    for band in bands(faces, zfull.shape[0]):
        rows = dual[...] if band.start == 0 else inner[band.start - face_rows:band.stop - face_rows, :]
        yield band, jnp.dot(rows, field, preferred_element_type=F32).astype(BF16)


def gather(field, zfull, tab, faces):
    t = Table(faces)
    order = zfull.shape[0]
    face_rows = faces * FACE_ROWS
    for f in range(faces):
        own = field[f * FACE_ROWS:(f + 1) * FACE_ROWS, :].astype(BF16).astype(F32)
        far = field[order + f * FACE_ROWS:order + (f + 1) * FACE_ROWS, :].astype(BF16).astype(F32)
        zfull[f * FACE_ROWS:(f + 1) * FACE_ROWS, :] = (own + tab[t.sign + f].astype(F32) * far).astype(BF16)
    zfull[face_rows:, :] = field[face_rows:order, :].astype(BF16)


def first_kernel(faces, groups, tab_v, lam_h, own_t, own_slab, dual_h, loads_h, *rest):
    recvs, (lam_all, all_t, zfull, image, dual, loads, choice), rest = rest[:SWAPS], rest[SWAPS:SWAPS + 7], rest[SWAPS + 7:]
    sends, rest = rest[:len(SENDS)], rest[len(SENDS):]
    pieces, (joined, slabs, picked, tab, sems) = rest[:groups], rest[groups:]
    t = Table(faces)
    order, columns = lam_h.shape
    block = CAP * FACE_ROWS
    face_rows = faces * FACE_ROWS
    made = copies(
        ((tab_v, tab), (lam_h, lam_all.at[0:order]), (dual_h.at[0, 0:face_rows], dual), (loads_h.at[0:face_rows], loads)), sems)
    for m, recv in zip(DIRECT, recvs):
        joined[m * FIRST_ROWS:(m + 1) * FIRST_ROWS, :] = recv[0:FIRST_ROWS, :]
    all_t[0:order, :] = own_t[...]
    made[0].wait()
    lanes = all_t.shape[1]
    lane = lax.broadcasted_iota(jnp.int32, (FACE_ROWS, lanes), 1)
    for f in range(faces):
        slot = tab[t.slot + f]
        turn = lax.rem(slot, CAP)
        start = lax.div(slot, CAP) * (2 * CAP + 1)
        high = joined[rows_of(start + turn), :].astype(F32)
        low = joined[rows_of(start + CAP + turn), :].astype(F32)
        at = order + f * FACE_ROWS
        lam_all[at:at + FACE_ROWS, :] = high + low
        side = joined[rows_of(start + 2 * CAP), :].astype(F32)
        mine = side
        for j in range(1, CAP):
            mine = jnp.where(turn == j, pltpu.roll(side, lanes - SIDE * j, 1), mine)
        high = jnp.where(lane < PAD, mine, 0.0)
        low = jnp.where((lane >= PAD) & (lane < 2 * PAD), mine, 0.0)
        flags = jnp.where((lane >= 2 * PAD) & (lane < 3 * PAD), mine, 0.0)
        trio = high + pltpu.roll(high, PAD, 1) + pltpu.roll(low, PAD, 1)
        placed = pltpu.roll(flags, CONTACT_LANE - 2 * PAD, 1)
        for i in range(len(OFFSETS)):
            moved = pltpu.roll(trio, GROUP * (1 + i), 1)
            placed = placed + jnp.where(tab[t.offset + f] == i, moved, 0.0)
        all_t[at:at + FACE_ROWS, :] = placed.astype(BF16)
    height, width = own_slab.shape
    slabs[0] = own_slab[...].astype(F32)
    for m, recv in zip(DIRECT, recvs):
        parts_in = [recv[FIRST_ROWS + k * height:FIRST_ROWS + (k + 1) * height, :] for k in range(width // 128)]
        slabs[1 + tab[t.which + m]] = jnp.concatenate(parts_in, axis=1).astype(F32)
    for i, piece in enumerate(pieces):
        group = lax.rem(tab[t.here + 1] + i, groups)
        picked[...] = jnp.zeros_like(picked)
        for k in range(len(NEAR)):
            picked[k * PAD:(k + 1) * PAD, :] = slabs[k, pl.ds(pl.multiple_of(group * PAD, PAD), PAD), :]
        piece[...] = picked[...].astype(BF16)
    slot = lax.broadcasted_iota(jnp.int32, choice.shape, 1)
    line = lax.broadcasted_iota(jnp.int32, choice.shape, 0)
    inside = lax.rem(slot, FACE_ROWS)
    chosen = jnp.zeros(choice.shape, jnp.int32)
    for q in range(SWAPS * CAP):
        values = jnp.where(line == 0, tab[t.far_block + q] * FACE_ROWS + inside, tab[t.far_sign + q])
        chosen = jnp.where(lax.div(slot, FACE_ROWS) == q, values, chosen)
    choice[...] = chosen.astype(F32)
    made[1].wait()
    gather(lam_all, zfull, tab, faces)
    made[2].wait()
    image[...] = jnp.dot(dual[...], zfull[...], preferred_element_type=F32).astype(BF16)
    pack(sends, image, tab, t.own_face)
    made[3].wait()


def step_length(parts):
    sums = jnp.sum(parts[...], axis=0)
    return sums[0:1, :] / sums[1:2, :]


def stepped(alpha, lam, dirn, all_t, step, rows):
    value = lam[rows, :] - alpha * dirn[rows, :]
    lane = CONTACT_LANE + step
    active = all_t[rows, lane:lane + 1].astype(F32)
    return jnp.where(active > 0.5, jnp.maximum(value, 0.0), value)


def update_kernel(faces, step, tab_v, dual, parts, lam_all, dirn_all, all_t, lam_next, zfull, image, *rest):
    sends, (tab, sems) = rest[:len(SENDS)], rest[len(SENDS):]
    (enter,) = copies(((tab_v, tab),), sems)
    lam_next[...] = stepped(step_length(parts), lam_all, dirn_all, all_t, step, slice(0, lam_all.shape[0]))
    enter.wait()
    gather(lam_next, zfull, tab, faces)
    image[...] = jnp.dot(dual[...], zfull[...], preferred_element_type=F32).astype(BF16)
    pack(sends, image, tab, Table(faces).own_face)


def residual_of(rows, grad):
    high, low = split(grad)
    columns = grad.shape[1]
    prod = jnp.dot(rows, jnp.concatenate([high, low], axis=1), preferred_element_type=F32)
    return prod[0:PAD, 0:columns] + (prod[PAD:2 * PAD, 0:columns] + prod[0:PAD, columns:2 * columns])


def inner_kernel(faces, dual_h, loads_h, zfull, rows, grad, residual, dual, loads, sems):
    order = zfull.shape[0]
    inner = bands(faces, order)[1:]
    face_rows = faces * FACE_ROWS
    made = fetch(dual_h, dual, sems, faces)
    (enter,) = copies(((loads_h.at[face_rows:order], loads),), sems.at[len(made):])
    field = zfull[...]
    enter.wait()
    for copy, band in zip(made, inner):
        copy.wait()
        here = slice(band.start - face_rows, band.stop - face_rows)
        image = jnp.dot(dual[here, :], field, preferred_element_type=F32).astype(BF16)
        grad[here, :] = image.astype(F32) - loads[here, :]
    residual[...] = residual_of(rows[:, face_rows:], grad[...])


def last_kernel(faces, step, parts, lam, dirn, all_t, out_h, out, sems):
    alpha = step_length(parts)
    made = []
    for i, band in enumerate(bands(faces, out.shape[0])):
        out[band, :] = stepped(alpha, lam, dirn, all_t, step, band)
        made += copies([(out.at[band], out_h.at[band])], sems.at[i:])
    for copy in made:
        copy.wait()


def spread_kernel(faces, first, counts, tab_v, choice, image, loads, rows, part, *rest):
    if first:
        pieces, rest = rest[:counts[1]], rest[counts[1]:]
    recvs, (grad, pay_h), rest = rest[:SWAPS], rest[SWAPS:SWAPS + 2], rest[SWAPS + 2:]
    sends, rest = rest[:len(SENDS)], rest[len(SENDS):]
    if first:
        inverse, rest = rest[0], rest[1:]
    if first:
        sorted_, rest = rest[0], rest[1:]
    low_grad, pay, tab, sems = rest
    (enter,) = copies(((tab_v, tab),), sems)
    t = Table(faces)
    n_sub, n_grp = counts
    face_rows = faces * FACE_ROWS
    columns = loads.shape[1]
    line = lax.broadcasted_iota(jnp.int32, (face_rows, choice.shape[1]), 0).astype(F32)
    select = jnp.where(line == choice[0:1, :], choice[1:2, :], 0.0).astype(BF16)
    came = jnp.concatenate([recv[0:CAP * FACE_ROWS, :] for recv in recvs], axis=0)
    returned = jnp.dot(select, came, preferred_element_type=F32)
    grad[...] = image[...].astype(F32) - loads[...] + returned
    low_grad[...] = grad[...].astype(BF16)
    residual = part[...] + residual_of(rows[:, 0:face_rows], grad[...])

    spread_out(jnp.broadcast_to(residual[None], (n_grp,) + residual.shape), pay, counts)
    (leave,) = copies(((pay, pay_h),), sems.at[1:])
    enter.wait()
    pack(sends, low_grad, tab, t.far_block)
    if first:
        inverse[...] = inverse_rows(pieces, tab[t.here + 1], sorted_)
    leave.wait()


def inverse_rows(pieces, group, ordered):
    groups = len(pieces)
    for i, piece in enumerate(pieces):
        ordered[lax.rem(group + groups - i, groups)] = piece[...].astype(F32)
    width = ordered.shape[2]
    blocks = [ordered[g, :, k:k + 128] for g in range(groups) for k in range(0, width, 128)]
    lane = lax.broadcasted_iota(jnp.int32, blocks[0].shape, 1)
    pairs = list(zip(blocks[0::2], blocks[1::2]))
    high = [jnp.where(lane < HALF, one, pltpu.roll(two, HALF, 1)) for one, two in pairs]
    low = [jnp.where(lane < HALF, pltpu.roll(one, HALF, 1), two) for one, two in pairs]
    return jnp.concatenate(high + high + low, axis=1).astype(BF16)


def direction_kernel(faces, tab_v, dual_h, dual, near, grad, grad_in, every, all_t, *rest):
    (far, passed, beside), rest = rest[:SWAPS - 1], rest[SWAPS - 1:]
    recvs = far, near, passed, beside
    (inverse, dirn, parts), rest = rest[:3], rest[3:]
    zfull, joined, grad_all, moved, tab, sems = rest
    (enter,) = copies(((tab_v, tab),), sems)
    made = fetch(dual_h, moved, sems.at[1:], faces)
    t = Table(faces)
    columns = grad.shape[1]
    order = grad.shape[0] + grad_in.shape[0]
    face_rows = faces * FACE_ROWS
    block = CAP * FACE_ROWS
    residual = every[...].reshape(every.shape[0] * PAD, columns)
    high, low = split(residual)
    stacked = jnp.concatenate([high, low, high], axis=0)
    corr = jnp.dot(inverse[...], stacked, preferred_element_type=F32)
    pieces = []
    for k in range(len(NEAR)):
        high, low = split(corr[k * PAD:(k + 1) * PAD, :])
        pieces += [high.astype(F32), low.astype(F32), high.astype(F32)]
    pieces.append(jnp.zeros((all_t.shape[1] - CONTACT_LANE, columns), F32))
    weights = jnp.concatenate(pieces, axis=0).astype(BF16)
    shift = jnp.dot(all_t[...], weights, preferred_element_type=F32)
    dirn[0:face_rows, :] = grad[...] - shift[0:face_rows, :]
    dirn[face_rows:order, :] = grad_in[...] - shift[face_rows:order, :]
    for m, recv in enumerate(recvs):
        joined[m * block:(m + 1) * block, :] = recv[0:block, :]
    enter.wait()
    for f in range(faces):
        at = f * FACE_ROWS
        grad_all[at:at + FACE_ROWS, :] = joined[rows_of(tab[t.slot + f]), :].astype(F32)
    dirn[order:, :] = grad_all[...] - shift[order:, :]
    gather(dirn, zfull, tab, faces)
    curv = jnp.zeros((1, columns), F32)
    for band, product in apply(made, dual, moved, zfull, faces):
        image = product.astype(F32)
        if band.start > 0:
            curv = curv + jnp.sum(dirn[band, :] * image, axis=0, keepdims=True)
            continue
        for f in range(faces):
            at = f * FACE_ROWS
            far = dirn[order + at:order + at + FACE_ROWS, :]
            gathered = dirn[at:at + FACE_ROWS, :] + tab[t.sign + f].astype(F32) * far
            curv = curv + jnp.sum(gathered * image[at:at + FACE_ROWS, :], axis=0, keepdims=True)
    slope = jnp.sum(grad[...] * dirn[0:face_rows, :], axis=0, keepdims=True)
    slope = slope + jnp.sum(grad_in[...] * dirn[face_rows:order, :], axis=0, keepdims=True)
    both = jnp.concatenate([slope, curv], axis=0)
    parts[...] = jnp.broadcast_to(both[None], parts.shape)


SMEM = pltpu.SMEM
VMEM = pltpu.VMEM
HBM = pltpu.HBM


def call(kernel, name, args, outs, scratch=(), scalars=(), copying=0, cost=None):
    size = 0
    held = [(a.shape, a.dtype) for a, space in args if space == VMEM] + [o[:2] for o in outs if o[2] == VMEM]
    for shape, dtype in held + list(scratch):
        shape = (1,) * (2 - len(shape)) + tuple(shape)
        padded = shape[:-2] + (-(-shape[-2] // 16) * 16, -(-shape[-1] // 128) * 128)
        count = jnp.dtype(dtype).itemsize
        for length in padded:
            count *= length
        size += count
    return pl.pallas_call(
        kernel,
        name=name,
        out_shape=[(HBM if space == HBM else jax.ShapeDtypeStruct)(shape, dtype) for shape, dtype, space in outs],
        in_specs=[pl.BlockSpec(memory_space=space) for _, space in args],
        out_specs=[pl.BlockSpec(memory_space=space) for _, _, space in outs],
        scratch_shapes=[pltpu.VMEM(shape, dtype) for shape, dtype in scratch]
        + [pltpu.SMEM(shape, dtype) for shape, dtype in scalars]
        + ([pltpu.SemaphoreType.DMA((copying,))] if copying else []),
        compiler_params=pltpu.CompilerParams(vmem_limit_bytes=size + (6 << 20)),
        cost_estimate=cost,
    )(*[a for a, _ in args])


def vmem(*arrays):
    return [(a, VMEM) for a in arrays]


def hbm(*arrays):
    return [(pltpu.with_memory_space_constraint(a, HBM), HBM) for a in arrays]


def turn(value, ahead):
    count = lax.axis_size("grp")
    return lax.ppermute(value, "grp", [(g, (g + ahead) % count) for g in range(count)])


def exchange(value):
    return lax.all_to_all(value, ("sub", "grp"), 0, 0)


def on_device(
    lam_start, loads, dual_ops, modes, coarse_inverse, face_offset, face_block, face_sign, contact
):
    n_sub, n_grp = lax.axis_size("sub"), lax.axis_size("grp")
    counts = (n_sub, n_grp)
    everyone = n_sub * n_grp
    order, columns = lam_start.shape
    faces = face_offset.shape[-1]
    steps = contact.shape[0]
    halo = faces * FACE_ROWS
    block = CAP * FACE_ROWS
    t = Table(faces)
    modes_n = coarse_inverse.shape[0] // n_grp
    blocks = -(-(coarse_inverse.shape[1] // modes_n * PAD) // HALF)
    slab_shape = (PAD * n_grp, blocks * 128)
    piece = (COARSE, blocks * 128)
    lane = jnp.arange(128, dtype=jnp.int32)
    pos = jnp.where(lane == 0, lax.axis_index("sub"), jnp.where(lane == 1, lax.axis_index("grp"), 0)).astype(jnp.int32)
    flat = hbm(*[a.reshape(n_sub, faces) for a in (face_offset, face_block, face_sign)])
    sent = [((len(held) * block, columns), BF16, VMEM) for held in SENDS]

    tab, rows, own_t, own_slab, *sends = call(
        functools.partial(start_kernel, faces, steps, n_grp), "start",
        vmem(pos) + flat + hbm(lam_start, modes, contact, coarse_inverse),
        [((t.size,), jnp.int32, VMEM), ((2 * PAD, order), BF16, VMEM), ((order, 128), BF16, VMEM),
         (slab_shape, BF16, VMEM)]
        + [((FIRST_ROWS + slab_shape[0] * slab_shape[1] // 128, columns), BF16, VMEM)] * SWAPS,
        [((128, order), F32), ((order, 128), F32), (lam_start.shape, F32), (modes.shape, F32), (contact.shape, jnp.int32),
         (coarse_inverse.shape, F32)],
        [((n_sub, faces), jnp.int32)] * 3 + [((128,), jnp.int32), ((t.size,), jnp.int32)], 9,
    )
    recvs = swap_direct(sends)
    table = [((t.size,), jnp.int32)]
    matrix = ((order - halo, order), BF16)
    parts_n = order // halo
    lam_all, all_t, zfull, image, dual, face_loads, choice, *sends = call(
        functools.partial(first_kernel, faces, n_grp), "first",
        vmem(tab) + hbm(lam_start) + vmem(own_t, own_slab) + hbm(dual_ops, loads) + vmem(*recvs),
        [((order + halo, columns), F32, VMEM), ((order + halo, 128), BF16, VMEM), ((order, columns), BF16, VMEM),
         ((halo, columns), BF16, VMEM), ((halo, order), BF16, VMEM),
         ((halo, columns), F32, VMEM), ((8, SWAPS * block), F32, VMEM)] + sent
        + [(piece, BF16, VMEM)] * n_grp,
        [((SWAPS * FIRST_ROWS, columns), BF16), ((len(NEAR),) + slab_shape, F32), (piece, F32)], table, 4,
    )
    sends, pieces = sends[:len(SENDS)], sends[len(SENDS):]
    for step in range(steps):
        first = step == 0
        returned = swap_all(sends)
        grad_in, part = call(
            functools.partial(inner_kernel, faces), "inner",
            hbm(dual_ops, loads) + vmem(zfull, rows),
            [((order - halo, columns), F32, VMEM), ((PAD, columns), F32, VMEM)],
            [((order - halo, order), BF16), ((order - halo, columns), F32)], (), parts_n,
            pl.CostEstimate(flops=2 * (order - halo) * order * columns, transcendentals=0,
                            bytes_accessed=2 * (order - halo) * order),
        )
        if first:
            pieces = [pieces[0]] + [turn(value, i) for i, value in enumerate(pieces) if i]
        made = [((COARSE, 3 * PAD * everyone), BF16, VMEM)]
        grad, pay, *sends = call(
            functools.partial(spread_kernel, faces, first, counts), "spread",
            vmem(tab, choice, image, face_loads, rows, part, *(pieces if first else []), *returned),
            [((halo, columns), F32, VMEM), ((everyone, PAD, columns), F32, HBM)] + sent + (made if first else []),
            ([((n_grp,) + piece, F32)] if first else []) + [((halo, columns), BF16), ((everyone, PAD, columns), F32)], table, 2,
        )
        if first:
            inverse = sends.pop()
        far, near, passed, beside = swap_all(sends)
        every = exchange(pay)
        dirn, parts = call(
            functools.partial(direction_kernel, faces), "direction",
            vmem(tab) + hbm(dual_ops) + vmem(dual, near, grad, grad_in, every, all_t, far, passed, beside, inverse),
            [((order + halo, columns), F32, VMEM), ((everyone, 2, columns), F32, VMEM)],
            [((order, columns), BF16), ((SWAPS * block, columns), BF16), ((halo, columns), F32), matrix], table, parts_n,
        )
        parts = exchange(parts)
        if step < steps - 1:
            lam_all, zfull, image, *sends = call(
                functools.partial(update_kernel, faces, step), "update",
                vmem(tab, dual, parts, lam_all, dirn, all_t),
                [((order + halo, columns), F32, VMEM), ((order, columns), BF16, VMEM), ((halo, columns), BF16, VMEM)] + sent,
                [], table, 1,
            )
    return call(
        functools.partial(last_kernel, faces, steps - 1), "last",
        vmem(parts, lam_all, dirn, all_t),
        [((order, columns), F32, HBM)], [((order, columns), F32)], (), order // halo,
    )[0]


def solution(mesh):
    return jax.shard_map(
        on_device,
        mesh=mesh,
        in_specs=(
            P(("sub", "grp"), None),
            P(("sub", "grp"), None),
            P(("sub", "grp"), None, None),
            P(None, ("sub", "grp")),
            P("sub", "grp"),
            P(None, "grp", None),
            P(None, "grp", None),
            P(None, "grp", None),
            P(None, ("sub", "grp")),
        ),
        out_specs=P(("sub", "grp"), None),
        check_vma=False,
    )
```
